32 devices in a mesh: shuf: 4 (over y, core), key: 8 (over z, x).
Axes of the slice: x: 2, y: 2, z: 4, core: 2. Of those that a mesh axis runs over, the one named last changes fastest.
Arguments:
- embeddings: bfloat16 [4096, 1024], P(('shuf', 'key')), may hold values from -200 to 200
- labels: int32 [4096], P(('shuf', 'key')), may hold values from 0 to 255
- order: int32 [32, 128], P(('shuf', 'key')), may hold values from 0 to 127, each once within a row
- head_weight: bfloat16 [1024, 512], replicated, may hold values from -0.1875 to 0.1875
Outputs:
- grad_embeddings: bfloat16 [4096, 1024], P(('shuf', 'key'))
- grad_head: float32 [1024, 512], P('key')
The draws below stay inside these ranges and needn't reach their ends.
All inputs are finite; a program needn't handle non-finite values.
Results may differ from the reference program's by a relative error of at most 0.0075.
Values may be sent and summed in bfloat16 or wider, within the bound.
A program may use at most 64 MiB of HBM per device.

```python
import jax
import jax.numpy as jnp
from jax import lax

D = 1024
PROJ = 512
ROWS = 128
BATCH = 4096
CLASSES = 256
N_SHUF = 4
N_KEY = 8


def label_helper(key):
    return jax.random.randint(jax.random.fold_in(key, 11), (BATCH,), 0, CLASSES, dtype=jnp.int32)


def draw_labels(key, part):
    return label_helper(key)


def center_helper(key):
    family_count = max(CLASSES // 16, 1)
    family_of = jax.random.randint(jax.random.fold_in(key, 41), (CLASSES,), 0, family_count, dtype=jnp.int32)
    family_centers = jax.random.normal(jax.random.fold_in(key, 43), (family_count, D), jnp.float32)
    own_centers = jax.random.normal(jax.random.fold_in(key, 23), (CLASSES, D), jnp.float32)
    return 0.92 * family_centers[family_of] + 0.39 * own_centers


def draw_embeddings(key, part):
    class_ids = label_helper(key)
    centers = center_helper(key)
    noise = jax.random.normal(jax.random.fold_in(key, 29), (BATCH, D), jnp.float32)
    value = 1.5 * centers[class_ids] + noise
    value = jnp.clip(value, -200.0, 200.0)
    return value.astype(jnp.bfloat16)


def gaussian(rng, dims, deviation, reach, kind=jnp.bfloat16):
    values = deviation * jax.random.normal(rng, dims, jnp.float32)
    return jnp.clip(values, min=-reach, max=reach).astype(kind)


def setup_inputs(seed: int = 0) -> dict:
    streams_of = jax.random.split(jax.random.key(seed), 5)
    return {
        "embeddings": draw_embeddings(jax.random.fold_in(streams_of[4], 71), 0),
        "labels": draw_labels(jax.random.fold_in(streams_of[4], 71), 0),
        "order": jax.vmap(lambda own: jax.random.permutation(own, ROWS))(jax.random.split(streams_of[2], (N_SHUF * N_KEY))).reshape((N_SHUF * N_KEY, ROWS)).astype(jnp.int32),
        "head_weight": gaussian(streams_of[3], (D, PROJ), D ** -0.5, 0.1875),
    }


exponent_divisor = 0.1
loss_scale = 64.0
epsilon = 1e-06

def tile_terms(query_embeddings, anchor_labels, anchor_index, candidate_table, key_labels):
    cosine_score_table = lax.dot_general(query_embeddings, candidate_table, (((1,), (1,)), ((), ())), preferred_element_type=jnp.float32) / exponent_divisor
    column = jnp.arange(candidate_table.shape[0], dtype=jnp.int32)
    itself = anchor_index[:, None] == column[None, :]
    exponent = jnp.where(itself, 0.0, jnp.exp(cosine_score_table))
    positive = jnp.logical_and(anchor_labels[:, None] == key_labels[None, :], jnp.logical_not(itself)).astype(jnp.float32)
    return (exponent, positive)

def group_terms(grouped, group_labels, head_weight):
    projected = jnp.dot(grouped, head_weight, preferred_element_type=jnp.float32)
    row_norm = jnp.sqrt(lax.optimization_barrier(jnp.sum(projected * projected, axis=1, keepdims=True)) + epsilon)
    direction = projected / row_norm
    normed = direction.astype(jnp.bfloat16)
    cohort_extent = grouped.shape[0]
    block_count = cohort_extent // ROWS
    tile_starting_positions = jnp.arange(block_count, dtype=jnp.int32) * ROWS

    def first_block(offset):
        query_embeddings = lax.dynamic_slice_in_dim(normed, offset, ROWS, 0)
        anchor_labels = lax.dynamic_slice_in_dim(group_labels, offset, ROWS, 0)
        anchor_index = offset + jnp.arange(ROWS, dtype=jnp.int32)
        exponent, positive = tile_terms(query_embeddings, anchor_labels, anchor_index, normed, group_labels)
        return (lax.optimization_barrier(jnp.sum(exponent, axis=1)), lax.optimization_barrier(jnp.sum(positive, axis=1)))
    totals, counts = lax.map(first_block, tile_starting_positions)
    totals = totals.reshape(-1)
    counts = counts.reshape(-1)
    floor_count = jnp.maximum(counts, 1.0)
    soft_weight = loss_scale * counts / (floor_count * totals)
    pos_weight = loss_scale / floor_count

    def following_tile(offset):
        query_embeddings = lax.dynamic_slice_in_dim(normed, offset, ROWS, 0)
        anchor_labels = lax.dynamic_slice_in_dim(group_labels, offset, ROWS, 0)
        anchor_index = offset + jnp.arange(ROWS, dtype=jnp.int32)
        anchor_soft = lax.dynamic_slice_in_dim(soft_weight, offset, ROWS, 0)
        anchor_pos = lax.dynamic_slice_in_dim(pos_weight, offset, ROWS, 0)
        exponent, positive = tile_terms(query_embeddings, anchor_labels, anchor_index, normed, group_labels)
        coefficient = ((anchor_soft[:, None] + soft_weight[None, :]) * exponent - (anchor_pos[:, None] + pos_weight[None, :]) * positive).astype(jnp.bfloat16)
        return jnp.dot(coefficient, normed, preferred_element_type=jnp.float32)
    positive_pull_derivative = lax.map(following_tile, tile_starting_positions).reshape(cohort_extent, -1) / exponent_divisor
    along = lax.optimization_barrier(jnp.sum(direction * positive_pull_derivative, axis=1, keepdims=True))
    slopes = ((positive_pull_derivative - direction * along) / row_norm).astype(jnp.bfloat16)
    grad_rows = lax.dot_general(slopes, head_weight, (((1,), (1,)), ((), ())), preferred_element_type=jnp.float32).astype(jnp.bfloat16)
    head_part = lax.dot_general(grouped, slopes, (((0,), (0,)), ((), ())), preferred_element_type=jnp.float32)
    return (grad_rows, head_part)

def reference(embeddings, labels, order, head_weight):
    share_rows = ROWS // N_SHUF
    group_ids = jnp.arange(N_SHUF, dtype=jnp.int32)[:, None, None, None]
    key_ids = jnp.arange(N_KEY, dtype=jnp.int32)[None, :, None, None]
    source_ids = jnp.arange(N_SHUF, dtype=jnp.int32)[None, None, :, None]
    slot_ids = jnp.arange(share_rows, dtype=jnp.int32)[None, None, None, :]
    device_ids = source_ids * N_KEY + key_ids
    local_rows = order[device_ids, group_ids * share_rows + slot_ids]
    loader_rows = (device_ids * ROWS + local_rows).reshape(N_SHUF, N_KEY * ROWS).astype(jnp.int32)
    grad_embeddings = jnp.zeros_like(embeddings)
    grad_head = jnp.zeros((D, PROJ), jnp.float32)
    for group_id in range(N_SHUF):
        picked = loader_rows[group_id]
        grad_rows, head_part = group_terms(embeddings[picked], labels[picked], head_weight)
        grad_embeddings = grad_embeddings.at[picked].set(grad_rows)
        grad_head = grad_head + head_part
    return (grad_embeddings, grad_head / loss_scale)
```

```python
import functools

import jax
import jax.numpy as jnp
from jax import lax
from jax.experimental import pallas as pl
from jax.experimental.pallas import tpu as pltpu
from jax.sharding import PartitionSpec as P

MESH = pl.DeviceIdType.MESH
F32, BF16 = jnp.float32, jnp.bfloat16
exponent_divisor = 0.1
loss_scale = 64.0
epsilon = 1e-06
PARTS = 4


def nn(a, b):
    return lax.dot_general(a, b, (((1,), (0,)), ((), ())), preferred_element_type=F32)


def nt(a, b):
    return lax.dot_general(a, b, (((1,), (1,)), ((), ())), preferred_element_type=F32)


def tn(a, b):
    return lax.dot_general(a, b, (((0,), (0,)), ((), ())), preferred_element_type=F32)


def kernel(
    m, emb_ref, lab_ref, order_ref, head_ref, gemb_ref, ghead_ref,
    slot_ref, group_ref, dir_ref, labs_ref, labz_ref, labg_ref, wts_ref, wtg_ref, exp_ref,
    tan_ref, tanz_ref, alongs_ref, alongz_ref, embt_ref, embg_ref, slq_ref, slg_ref,
    hs_ref, hz_ref, qs_ref, qg_ref,
    zs_sem, zr_sem, lzs_sem, lzr_sem, lgs_sem, lgr_sem, wgs_sem, wgr_sem,
    gs_sem, gr_sem, gfs_sem, gfr_sem, es_sem, er_sem, efs_sem, efr_sem,
    ts_sem, tr_sem, as_sem, ar_sem, ss_sem, sr_sem, hs_sem, hr_sem, qs_sem, qr_sem,
):
    rows, width = emb_ref.shape
    slab = rows // PARTS
    nk = PARTS * m
    dk = width // nk
    quarter = head_ref.shape[1] // PARTS
    u = lax.axis_index("shuf")
    k = lax.axis_index("key")
    z, j = k // m, k % m

    def flip(a, du):
        for bit in (1, 2):
            if du & bit:
                a = a + bit - 2 * bit * ((a // bit) % 2)
        return a

    def ahead(dz):
        return (z + dz) % PARTS

    def behind(dz):
        return (z + PARTS - dz) % PARTS

    def there(du, dj):
        return flip(u, du), (j + dj) % m

    def origin(du, dj):
        return flip(u, du), (j + m - dj) % m

    def block_of(uj):
        return uj[0] * m + uj[1]

    def block_rows(ref, b):
        return ref.at[pl.ds(pl.multiple_of(b * rows, rows), rows)]

    def plane_id(uj):
        return (uj[0], z * m + uj[1])

    def z_id(zz):
        return (u, zz * m + j)

    pending = []

    def send(src, dst, s_sem, r_sem, to):
        copy = pltpu.make_async_remote_copy(
            src_ref=src, dst_ref=dst, send_sem=s_sem, recv_sem=r_sem, device_id=to, device_id_type=MESH
        )
        copy.start()
        pending.append(copy)

    def arrived(dst, s_sem, r_sem, frm):
        pltpu.make_async_remote_copy(
            src_ref=dst, dst_ref=dst, send_sem=s_sem, recv_sem=r_sem, device_id=frm, device_id_type=MESH
        ).wait_recv()

    same_core = [(du, dj) for dj in range(m) for du in (0, 2)]
    plane = [(du, dj) for dj in range(m) for du in range(PARTS)]
    mine = block_of((u, j))

    barrier = pltpu.get_barrier_semaphore()
    for off in plane[1:]:
        pl.semaphore_signal(barrier, inc=1, device_id=plane_id(there(*off)), device_id_type=MESH)
    for dz in range(1, PARTS):
        pl.semaphore_signal(barrier, inc=1, device_id=z_id(ahead(dz)), device_id_type=MESH)

    sub = lax.broadcasted_iota(jnp.int32, (rows, rows), 0)
    lane = lax.broadcasted_iota(jnp.int32, (rows, rows), 1)
    eye = sub == lane
    place = sub == order_ref[...]
    place_bf = place.astype(F32).astype(BF16)

    projected = nn(emb_ref[...], head_ref[...])
    row_norm = jnp.sqrt(jnp.sum(projected * projected, axis=1, keepdims=True) + epsilon)
    direction = projected / row_norm
    dir_ref[...] = direction
    normed = direction.astype(BF16)
    slot_ref[...] = tn(place_bf, normed).astype(BF16)

    def column(row):
        return jnp.sum(jnp.where(eye, row, 0.0), axis=1, keepdims=True)

    def row_of(col):
        return jnp.sum(jnp.where(eye, col, 0.0), axis=0, keepdims=True)

    lab_col = column(lab_ref[...].astype(F32))
    lab_slot = jnp.sum(jnp.where(place, lab_col, 0.0), axis=0, keepdims=True)
    labs_ref[...] = jnp.broadcast_to(lab_slot, labs_ref.shape)
    pl.semaphore_wait(barrier, nk - 1 + PARTS - 1)

    def slab_rows(ref, i):
        return ref.at[pl.ds(pl.multiple_of(i * slab, slab), slab)]

    def group_slab(b, i):
        return group_ref.at[pl.ds(pl.multiple_of(b * rows + i * slab, slab), slab)]

    for dz in range(1, PARTS):
        zz = ahead(dz)
        send(labs_ref, labz_ref.at[z], lzs_sem.at[dz], lzr_sem.at[dz], z_id(zz))
        send(slab_rows(slot_ref, zz), group_slab(mine, z), zs_sem.at[dz], zr_sem.at[dz], z_id(zz))
    own = pl.multiple_of(mine * rows + z * slab, slab)
    group_ref[pl.ds(own, slab), :] = slot_ref[pl.ds(pl.multiple_of(z * slab, slab), slab), :]
    labz_ref[z] = labs_ref[...]

    turned = emb_ref[...].T
    for jj in range(m):
        for zz in range(PARTS):
            first = (zz * m + jj) * dk
            embt_ref[jj, zz * dk : (zz + 1) * dk, :] = turned[first : first + dk, :]
    for i, off in enumerate(same_core):
        if i:
            to = there(*off)
            send(embt_ref.at[to[1]], embg_ref.at[mine], es_sem.at[i], er_sem.at[i], plane_id(to))
    embg_ref[mine] = embt_ref[j]

    def extract(buf_ref):
        lanes = lax.broadcasted_iota(jnp.int32, (8, rows), 1) // slab
        out = jnp.zeros((8, rows), F32)
        for i in range(PARTS):
            moved = pltpu.roll(buf_ref[i], ((i + PARTS - z) % PARTS) * slab, 1)
            out = jnp.where(lanes == i, moved, out)
        return out

    for dz in range(1, PARTS):
        arrived(group_slab(mine, behind(dz)), zs_sem.at[dz], zr_sem.at[dz], z_id(behind(dz)))
    for i, off in enumerate(same_core):
        if i:
            to = there(*off)
            send(block_rows(group_ref, mine), block_rows(group_ref, mine), gs_sem.at[i], gr_sem.at[i], plane_id(to))
    partner = there(1, 0)
    send(block_rows(group_ref, mine), block_rows(group_ref, mine), gfs_sem.at[0], gfr_sem.at[0], plane_id(partner))
    for dz in range(1, PARTS):
        arrived(labz_ref.at[behind(dz)], lzs_sem.at[dz], lzr_sem.at[dz], z_id(behind(dz)))
    labg_ref[mine] = extract(labz_ref)
    for i, off in enumerate(plane):
        if i:
            send(labg_ref.at[mine], labg_ref.at[mine], lgs_sem.at[i], lgr_sem.at[i], plane_id(there(*off)))

    def load_block(b):
        return group_ref[pl.ds(pl.multiple_of(b * rows, rows), rows), :]

    anchors = load_block(mine)
    anchor_col = column(labg_ref[mine][0:1, :])

    def exponent_of(i, b):
        value = jnp.exp(nt(anchors, load_block(b)) / exponent_divisor)
        if i == 0:
            value = jnp.where(eye, 0.0, value)
        exp_ref[i] = value
        return value

    def positive_of(i, b):
        same = anchor_col == labg_ref[b][0:1, :]
        if i == 0:
            same = jnp.logical_and(same, jnp.logical_not(eye))
        return jnp.where(same, 1.0, 0.0)

    total = exponent_of(0, mine)
    blocks = [mine]
    for i, off in enumerate(same_core):
        if i:
            frm = origin(*off)
            b = block_of(frm)
            arrived(block_rows(group_ref, b), gs_sem.at[i], gr_sem.at[i], plane_id(frm))
            send(block_rows(group_ref, b), block_rows(group_ref, b), gfs_sem.at[i], gfr_sem.at[i], plane_id(partner))
            total = total + exponent_of(len(blocks), b)
            blocks.append(b)
    for i, off in enumerate(plane):
        if i:
            frm = origin(*off)
            arrived(labg_ref.at[block_of(frm)], lgs_sem.at[i], lgr_sem.at[i], plane_id(frm))
    forwarded = []
    for i, off in enumerate(same_core):
        uj = origin(*off)
        forwarded.append(block_of((flip(uj[0], 1), uj[1])))
    for i, b in enumerate(forwarded):
        arrived(block_rows(group_ref, b), gfs_sem.at[i], gfr_sem.at[i], plane_id(partner))
        total = total + exponent_of(len(blocks), b)
        blocks.append(b)
    positive = positive_of(0, mine)
    for i in range(1, nk):
        positive = positive + positive_of(i, blocks[i])
    totals = jnp.sum(total, axis=1, keepdims=True)
    counts = jnp.sum(positive, axis=1, keepdims=True)
    floor_count = jnp.maximum(counts, 1.0)
    soft = loss_scale * counts / (floor_count * totals)
    pos = loss_scale / floor_count
    first_row = lax.broadcasted_iota(jnp.int32, (8, rows), 0) == 0
    wts_ref[...] = jnp.where(first_row, row_of(soft), row_of(pos))
    wtg_ref[mine] = wts_ref[...]
    for i, off in enumerate(plane):
        if i:
            send(wts_ref, wtg_ref.at[mine], wgs_sem.at[i], wgr_sem.at[i], plane_id(there(*off)))

    for i, off in enumerate(same_core):
        frm = origin(*off)
        b = block_of(frm)
        if i:
            arrived(embg_ref.at[b], es_sem.at[i], er_sem.at[i], plane_id(frm))
        send(embg_ref.at[b], embg_ref.at[b], efs_sem.at[i], efr_sem.at[i], plane_id(partner))

    for i, off in enumerate(plane):
        if i:
            frm = origin(*off)
            arrived(wtg_ref.at[block_of(frm)], wgs_sem.at[i], wgr_sem.at[i], plane_id(frm))
    pull = jnp.zeros((rows, head_ref.shape[1]), F32)
    for i, b in enumerate(blocks):
        weights = wtg_ref[b]
        coefficient = (soft + weights[0:1, :]) * exp_ref[i] - (pos + weights[1:2, :]) * positive_of(i, b)
        pull = pull + nn(coefficient.astype(BF16), load_block(b))
    pull = pull / exponent_divisor
    anchors32 = anchors.astype(F32)
    along = jnp.sum(anchors32 * pull, axis=1, keepdims=True)
    tan_ref[...] = (pull - anchors32 * along).astype(BF16)
    alongs_ref[...] = jnp.broadcast_to(row_of(along), alongs_ref.shape)
    for dz in range(1, PARTS):
        zz = ahead(dz)
        send(slab_rows(tan_ref, zz), slab_rows(tanz_ref, z), ts_sem.at[dz], tr_sem.at[dz], z_id(zz))
        send(alongs_ref, alongz_ref.at[z], as_sem.at[dz], ar_sem.at[dz], z_id(zz))
    own = pl.multiple_of(z * slab, slab)
    tanz_ref[pl.ds(own, slab), :] = tan_ref[pl.ds(own, slab), :]
    alongz_ref[z] = alongs_ref[...]
    for dz in range(1, PARTS):
        frm = behind(dz)
        arrived(slab_rows(tanz_ref, frm), ts_sem.at[dz], tr_sem.at[dz], z_id(frm))
        arrived(alongz_ref.at[frm], as_sem.at[dz], ar_sem.at[dz], z_id(frm))

    direction = dir_ref[...]
    along = jnp.sum(jnp.where(place, extract(alongz_ref)[0:1, :], 0.0), axis=1, keepdims=True)
    pull = nn(place_bf, tanz_ref[...]) + along * direction.astype(BF16).astype(F32)
    slopes = (pull - direction * jnp.sum(direction * pull, axis=1, keepdims=True)) / row_norm
    slopes = slopes.astype(BF16)
    for uu in range(PARTS):
        slq_ref[uu] = slopes[:, uu * quarter : (uu + 1) * quarter]
    for i, off in enumerate(plane):
        if i:
            to = there(*off)
            send(slq_ref.at[to[0]], slg_ref.at[mine], ss_sem.at[i], sr_sem.at[i], plane_id(to))
    slg_ref[mine] = slq_ref[u]
    gemb_ref[...] = nt(slopes, head_ref[...]).astype(BF16)
    for i, b in enumerate(forwarded):
        arrived(embg_ref.at[b], efs_sem.at[i], efr_sem.at[i], plane_id(partner))
    part = nn(embg_ref[mine], slg_ref[mine])
    for i, off in enumerate(plane):
        if i:
            frm = origin(*off)
            b = block_of(frm)
            arrived(slg_ref.at[b], ss_sem.at[i], sr_sem.at[i], plane_id(frm))
            part = part + nn(embg_ref[b], slg_ref[b])
    hs_ref[...] = part.astype(BF16).reshape(hs_ref.shape)
    for dz in range(1, PARTS):
        zz = ahead(dz)
        send(hs_ref.at[zz], hz_ref.at[z], hs_sem.at[dz], hr_sem.at[dz], z_id(zz))
    hz_ref[z] = hs_ref[z]
    for dz in range(1, PARTS):
        arrived(hz_ref.at[behind(dz)], hs_sem.at[dz], hr_sem.at[dz], z_id(behind(dz)))
    part = hz_ref[0].astype(F32)
    for zz in range(1, PARTS):
        part = part + hz_ref[zz].astype(F32)
    qs_ref[...] = part / loss_scale
    for du in range(1, PARTS):
        send(qs_ref, qg_ref.at[u], qs_sem.at[du], qr_sem.at[du], plane_id(there(du, 0)))
    qg_ref[u] = qs_ref[...]
    for du in range(1, PARTS):
        frm = origin(du, 0)
        arrived(qg_ref.at[frm[0]], qs_sem.at[du], qr_sem.at[du], plane_id(frm))
    for uu in range(PARTS):
        ghead_ref[:, uu * quarter : (uu + 1) * quarter] = qg_ref[uu]
    for copy in pending:
        copy.wait_send()


def body(m, embeddings, labels, order, head_weight):
    rows, width = embeddings.shape
    proj = head_weight.shape[1]
    nk = PARTS * m
    dk = width // nk
    quarter = proj // PARTS
    vmem = pltpu.VMEM
    scratch = [
        vmem((rows, proj), BF16),
        vmem((nk * rows, proj), BF16),
        vmem((rows, proj), F32),
        vmem((8, rows), F32),
        vmem((PARTS, 8, rows), F32),
        vmem((nk, 8, rows), F32),
        vmem((8, rows), F32),
        vmem((nk, 8, rows), F32),
        vmem((nk, rows, rows), F32),
        vmem((rows, proj), BF16),
        vmem((rows, proj), BF16),
        vmem((8, rows), F32),
        vmem((PARTS, 8, rows), F32),
        vmem((m, PARTS * dk, rows), BF16),
        vmem((nk, PARTS * dk, rows), BF16),
        vmem((PARTS, rows, quarter), BF16),
        vmem((nk, rows, quarter), BF16),
        vmem((PARTS, dk, quarter), BF16),
        vmem((PARTS, dk, quarter), BF16),
        vmem((dk, quarter), F32),
        vmem((PARTS, dk, quarter), F32),
    ]
    four, core, full = PARTS, 2 * m, nk
    for count in (four, four, full, full, core, core, core, core, four, four, full, four, four):
        scratch += [pltpu.SemaphoreType.DMA((count,))] * 2
    macs = rows * proj * (2 * width + 2 * nk * rows) + PARTS * dk * nk * rows * quarter
    return pl.pallas_call(
        functools.partial(kernel, m),
        out_shape=(
            jax.ShapeDtypeStruct((rows, width), BF16),
            jax.ShapeDtypeStruct((dk, proj), F32),
        ),
        in_specs=[pl.BlockSpec(memory_space=pltpu.VMEM)] * 4,
        out_specs=(pl.BlockSpec(memory_space=pltpu.VMEM), pl.BlockSpec(memory_space=pltpu.VMEM)),
        scratch_shapes=scratch,
        cost_estimate=pl.CostEstimate(flops=2 * macs, bytes_accessed=4 * rows * width + 2 * width * proj, transcendentals=rows * rows * nk),
        compiler_params=pltpu.CompilerParams(
            collective_id=0, has_side_effects=True, vmem_limit_bytes=48 * 1024 * 1024
        ),
    )(embeddings, labels.reshape(1, rows), order, head_weight)


def solution(mesh):
    m = mesh.shape["key"] // PARTS
    return jax.shard_map(
        functools.partial(body, m),
        mesh=mesh,
        in_specs=(P(("shuf", "key"), None), P(("shuf", "key")), P(("shuf", "key"), None), P()),
        out_specs=(P(("shuf", "key"), None), P("key", None)),
        check_vma=False,
    )
```

```python
import functools

import jax
import jax.numpy as jnp
from jax import lax
from jax.experimental import pallas as pl
from jax.experimental.pallas import tpu as pltpu
from jax.sharding import PartitionSpec as P

MESH = pl.DeviceIdType.MESH
F32, BF16 = jnp.float32, jnp.bfloat16
exponent_divisor = 0.1
loss_scale = 64.0
epsilon = 1e-06
PARTS = 4


def nn(a, b):
    return lax.dot_general(a, b, (((1,), (0,)), ((), ())), preferred_element_type=F32)


def nt(a, b):
    return lax.dot_general(a, b, (((1,), (1,)), ((), ())), preferred_element_type=F32)


def tn(a, b):
    return lax.dot_general(a, b, (((0,), (0,)), ((), ())), preferred_element_type=F32)


def kernel(
    m, emb_hbm, lab_hbm, order_hbm, head_hbm, gemb_ref, ghead_ref,
    emb_ref, lab_ref, order_ref, head_ref,
    slot_ref, group_ref, labs_ref, labz_ref, labg_ref, wts_ref, wtg_ref, exp_ref,
    embs_ref, embz_ref, slope_ref, slopez_ref, embt_ref, embg_ref, slq_ref, slg_ref,
    hs_ref, hz_ref, qs_ref, qg_ref,
    in_sem, zs_sem, zr_sem, lzs_sem, lzr_sem, lgs_sem, lgr_sem, wgs_sem, wgr_sem,
    gs_sem, gr_sem, gfs_sem, gfr_sem, es_sem, er_sem, efs_sem, efr_sem,
    ts_sem, tr_sem, cs_sem, cr_sem, ss_sem, sr_sem, hs_sem, hr_sem, qs_sem, qr_sem,
):
    rows, width = emb_ref.shape
    slab = rows // PARTS
    nk = PARTS * m
    dk = width // nk
    quarter = head_ref.shape[1] // PARTS
    u = lax.axis_index("shuf")
    k = lax.axis_index("key")
    z, j = k // m, k % m

    def flip(a, du):
        for bit in (1, 2):
            if du & bit:
                a = a + bit - 2 * bit * ((a // bit) % 2)
        return a

    def ahead(dz):
        return (z + dz) % PARTS

    def behind(dz):
        return (z + PARTS - dz) % PARTS

    def there(du, dj):
        return flip(u, du), (j + dj) % m

    def origin(du, dj):
        return flip(u, du), (j + m - dj) % m

    def block_of(uj):
        return uj[0] * m + uj[1]

    def block_rows(ref, b):
        return ref.at[pl.ds(pl.multiple_of(b * rows, rows), rows)]

    def plane_id(uj):
        return (uj[0], z * m + uj[1])

    def z_id(zz):
        return (u, zz * m + j)

    pending = []

    def send(src, dst, s_sem, r_sem, to):
        copy = pltpu.make_async_remote_copy(
            src_ref=src, dst_ref=dst, send_sem=s_sem, recv_sem=r_sem, device_id=to, device_id_type=MESH
        )
        copy.start()
        pending.append(copy)

    def arrived(dst, s_sem, r_sem, frm):
        pltpu.make_async_remote_copy(
            src_ref=dst, dst_ref=dst, send_sem=s_sem, recv_sem=r_sem, device_id=frm, device_id_type=MESH
        ).wait_recv()

    same_core = [(du, dj) for dj in range(m) for du in (0, 2)]
    plane = [(du, dj) for dj in range(m) for du in range(PARTS)]
    mine = block_of((u, j))

    loads = [
        pltpu.make_async_copy(src, dst, in_sem.at[i])
        for i, (src, dst) in enumerate(
            [(order_hbm, order_ref), (emb_hbm, emb_ref), (lab_hbm, lab_ref), (head_hbm, head_ref)]
        )
    ]
    for load in loads:
        load.start()
    barrier = pltpu.get_barrier_semaphore()
    for off in plane[1:]:
        pl.semaphore_signal(barrier, inc=1, device_id=plane_id(there(*off)), device_id_type=MESH)
    for dz in range(1, PARTS):
        pl.semaphore_signal(barrier, inc=1, device_id=z_id(ahead(dz)), device_id_type=MESH)

    sub = lax.broadcasted_iota(jnp.int32, (rows, rows), 0)
    lane = lax.broadcasted_iota(jnp.int32, (rows, rows), 1)
    eye = sub == lane
    loads[0].wait()
    place = sub == order_ref[...]
    place_bf = place.astype(F32).astype(BF16)

    def directions(x):
        projected = nn(x, head_ref[...])
        row_norm = jnp.sqrt(jnp.sum(projected * projected, axis=1, keepdims=True) + epsilon)
        return projected / row_norm, row_norm

    loads[1].wait()
    embs_ref[...] = tn(place_bf, emb_ref[...]).astype(BF16)
    loads[2].wait()
    loads[3].wait()
    slot_ref[...] = directions(embs_ref[...])[0].astype(BF16)

    def column(row):
        return jnp.sum(jnp.where(eye, row, 0.0), axis=1, keepdims=True)

    def row_of(col):
        return jnp.sum(jnp.where(eye, col, 0.0), axis=0, keepdims=True)

    lab_col = column(lab_ref[...].astype(F32))
    lab_slot = jnp.sum(jnp.where(place, lab_col, 0.0), axis=0, keepdims=True)
    labs_ref[...] = jnp.broadcast_to(lab_slot, labs_ref.shape)
    pl.semaphore_wait(barrier, nk - 1 + PARTS - 1)

    def slab_rows(ref, i):
        return ref.at[pl.ds(pl.multiple_of(i * slab, slab), slab)]

    def group_slab(b, i):
        return group_ref.at[pl.ds(pl.multiple_of(b * rows + i * slab, slab), slab)]

    for dz in range(1, PARTS):
        zz = ahead(dz)
        send(slab_rows(slot_ref, zz), group_slab(mine, z), zs_sem.at[dz], zr_sem.at[dz], z_id(zz))
    for dz in range(1, PARTS):
        send(labs_ref, labz_ref.at[z], lzs_sem.at[dz], lzr_sem.at[dz], z_id(ahead(dz)))
    own = pl.multiple_of(mine * rows + z * slab, slab)
    own_slot = pl.multiple_of(z * slab, slab)
    group_ref[pl.ds(own, slab), :] = slot_ref[pl.ds(own_slot, slab), :]
    labz_ref[z] = labs_ref[...]

    def extract(buf_ref):
        lanes = lax.broadcasted_iota(jnp.int32, (8, rows), 1) // slab
        out = jnp.zeros((8, rows), F32)
        for i in range(PARTS):
            moved = pltpu.roll(buf_ref[i], ((i + PARTS - z) % PARTS) * slab, 1)
            out = jnp.where(lanes == i, moved, out)
        return out

    for dz in range(PARTS):
        piece = group_slab(mine, behind(dz))
        if dz:
            arrived(piece, zs_sem.at[dz], zr_sem.at[dz], z_id(behind(dz)))
        for i, off in enumerate(same_core):
            if i:
                n = i * PARTS + dz
                send(piece, piece, gs_sem.at[n], gr_sem.at[n], plane_id(there(*off)))
    partner = there(1, 0)
    send(block_rows(group_ref, mine), block_rows(group_ref, mine), gfs_sem.at[0], gfr_sem.at[0], plane_id(partner))
    embz_ref[pl.ds(own_slot, slab), :] = embs_ref[pl.ds(own_slot, slab), :]
    for dz in range(1, PARTS):
        zz = ahead(dz)
        send(slab_rows(embs_ref, zz), slab_rows(embz_ref, z), cs_sem.at[dz], cr_sem.at[dz], z_id(zz))
    for dz in range(1, PARTS):
        arrived(labz_ref.at[behind(dz)], lzs_sem.at[dz], lzr_sem.at[dz], z_id(behind(dz)))
    labg_ref[mine] = extract(labz_ref)
    for i, off in enumerate(plane):
        if i:
            send(labg_ref.at[mine], labg_ref.at[mine], lgs_sem.at[i], lgr_sem.at[i], plane_id(there(*off)))

    def load_block(b):
        return group_ref[pl.ds(pl.multiple_of(b * rows, rows), rows), :]

    anchors = load_block(mine)
    anchor_col = column(labg_ref[mine][0:1, :])

    def exponent_of(i, b):
        value = jnp.exp(nt(anchors, load_block(b)) / exponent_divisor)
        if i == 0:
            value = jnp.where(eye, 0.0, value)
        exp_ref[i] = value
        return value

    def positive_of(i, b):
        same = anchor_col == labg_ref[b][0:1, :]
        if i == 0:
            same = jnp.logical_and(same, jnp.logical_not(eye))
        return jnp.where(same, 1.0, 0.0)

    total = exponent_of(0, mine)
    blocks = [mine]
    for i, off in enumerate(same_core):
        if i:
            frm = origin(*off)
            b = block_of(frm)
            for dz in range(PARTS):
                n = i * PARTS + dz
                arrived(group_slab(b, behind(dz)), gs_sem.at[n], gr_sem.at[n], plane_id(frm))
            send(block_rows(group_ref, b), block_rows(group_ref, b), gfs_sem.at[i], gfr_sem.at[i], plane_id(partner))
            total = total + exponent_of(len(blocks), b)
            blocks.append(b)
    for i, off in enumerate(plane):
        if i:
            frm = origin(*off)
            arrived(labg_ref.at[block_of(frm)], lgs_sem.at[i], lgr_sem.at[i], plane_id(frm))
    forwarded = []
    for i, off in enumerate(same_core):
        uj = origin(*off)
        forwarded.append(block_of((flip(uj[0], 1), uj[1])))
    for i, b in enumerate(forwarded):
        arrived(block_rows(group_ref, b), gfs_sem.at[i], gfr_sem.at[i], plane_id(partner))
        total = total + exponent_of(len(blocks), b)
        blocks.append(b)
    positive = positive_of(0, mine)
    for i in range(1, nk):
        positive = positive + positive_of(i, blocks[i])
    totals = jnp.sum(total, axis=1, keepdims=True)
    counts = jnp.sum(positive, axis=1, keepdims=True)
    floor_count = jnp.maximum(counts, 1.0)
    soft = loss_scale * counts / (floor_count * totals)
    pos = loss_scale / floor_count
    first_row = lax.broadcasted_iota(jnp.int32, (8, rows), 0) == 0
    wts_ref[...] = jnp.where(first_row, row_of(soft), row_of(pos))
    wtg_ref[mine] = wts_ref[...]
    for i, off in enumerate(plane):
        if i:
            send(wts_ref, wtg_ref.at[mine], wgs_sem.at[i], wgr_sem.at[i], plane_id(there(*off)))

    for dz in range(1, PARTS):
        arrived(slab_rows(embz_ref, behind(dz)), cs_sem.at[dz], cr_sem.at[dz], z_id(behind(dz)))
    turned = embz_ref[...].T
    for jj in range(m):
        for zz in range(PARTS):
            start = (zz * m + jj) * dk
            embt_ref[jj, zz * dk : (zz + 1) * dk, :] = turned[start : start + dk, :]
    for i, off in enumerate(same_core):
        if i:
            to = there(*off)
            send(embt_ref.at[to[1]], embg_ref.at[mine], es_sem.at[i], er_sem.at[i], plane_id(to))
    embg_ref[mine] = embt_ref[j]
    send(embg_ref.at[mine], embg_ref.at[mine], efs_sem.at[0], efr_sem.at[0], plane_id(partner))
    direction, row_norm = directions(embz_ref[...])

    for i, off in enumerate(plane):
        if i:
            frm = origin(*off)
            arrived(wtg_ref.at[block_of(frm)], wgs_sem.at[i], wgr_sem.at[i], plane_id(frm))
    pull = jnp.zeros((rows, head_ref.shape[1]), F32)
    for i, b in enumerate(blocks):
        weights = wtg_ref[b]
        coefficient = (soft + weights[0:1, :]) * exp_ref[i] - (pos + weights[1:2, :]) * positive_of(i, b)
        pull = pull + nn(coefficient.astype(BF16), load_block(b))
    pull = pull / exponent_divisor
    slopes = (pull - direction * jnp.sum(direction * pull, axis=1, keepdims=True)) / row_norm
    slopes = slopes.astype(BF16)
    slope_ref[...] = slopes
    for uu in range(PARTS):
        slq_ref[uu] = slopes[:, uu * quarter : (uu + 1) * quarter]
    for i, off in enumerate(plane):
        if i:
            to = there(*off)
            send(slq_ref.at[to[0]], slg_ref.at[mine], ss_sem.at[i], sr_sem.at[i], plane_id(to))
    slg_ref[mine] = slq_ref[u]
    for dz in range(1, PARTS):
        zz = ahead(dz)
        send(slab_rows(slope_ref, zz), slab_rows(slopez_ref, z), ts_sem.at[dz], tr_sem.at[dz], z_id(zz))
    slopez_ref[pl.ds(own_slot, slab), :] = slope_ref[pl.ds(own_slot, slab), :]
    for i, off in enumerate(same_core):
        if i:
            frm = origin(*off)
            b = block_of(frm)
            arrived(embg_ref.at[b], es_sem.at[i], er_sem.at[i], plane_id(frm))
            send(embg_ref.at[b], embg_ref.at[b], efs_sem.at[i], efr_sem.at[i], plane_id(partner))
    for i, b in enumerate(forwarded):
        arrived(embg_ref.at[b], efs_sem.at[i], efr_sem.at[i], plane_id(partner))
    part = nn(embg_ref[mine], slg_ref[mine])
    for i, off in enumerate(plane):
        if i:
            frm = origin(*off)
            b = block_of(frm)
            arrived(slg_ref.at[b], ss_sem.at[i], sr_sem.at[i], plane_id(frm))
            part = part + nn(embg_ref[b], slg_ref[b])
    hs_ref[...] = part.astype(BF16).reshape(hs_ref.shape)
    for dz in range(1, PARTS):
        zz = ahead(dz)
        send(hs_ref.at[zz], hz_ref.at[z], hs_sem.at[dz], hr_sem.at[dz], z_id(zz))
    hz_ref[z] = hs_ref[z]
    for dz in range(1, PARTS):
        frm = behind(dz)
        arrived(slab_rows(slopez_ref, frm), ts_sem.at[dz], tr_sem.at[dz], z_id(frm))
    gemb_ref[...] = nt(nn(place_bf, slopez_ref[...]).astype(BF16), head_ref[...]).astype(BF16)
    for dz in range(1, PARTS):
        arrived(hz_ref.at[behind(dz)], hs_sem.at[dz], hr_sem.at[dz], z_id(behind(dz)))
    part = hz_ref[0].astype(F32)
    for zz in range(1, PARTS):
        part = part + hz_ref[zz].astype(F32)
    qs_ref[...] = (part / loss_scale).astype(BF16)
    for du in range(1, PARTS):
        send(qs_ref, qg_ref.at[u], qs_sem.at[du], qr_sem.at[du], plane_id(there(du, 0)))
    qg_ref[u] = qs_ref[...]
    for du in range(1, PARTS):
        frm = origin(du, 0)
        arrived(qg_ref.at[frm[0]], qs_sem.at[du], qr_sem.at[du], plane_id(frm))
    for uu in range(PARTS):
        ghead_ref[:, uu * quarter : (uu + 1) * quarter] = qg_ref[uu].astype(F32)
    for copy in pending:
        copy.wait_send()


def body(m, embeddings, labels, order, head_weight):
    rows, width = embeddings.shape
    proj = head_weight.shape[1]
    nk = PARTS * m
    dk = width // nk
    quarter = proj // PARTS
    vmem = pltpu.VMEM
    scratch = [
        vmem((rows, width), BF16),
        vmem((1, rows), jnp.int32),
        vmem((1, rows), jnp.int32),
        vmem((width, proj), BF16),
        vmem((rows, proj), BF16),
        vmem((nk * rows, proj), BF16),
        vmem((8, rows), F32),
        vmem((PARTS, 8, rows), F32),
        vmem((nk, 8, rows), F32),
        vmem((8, rows), F32),
        vmem((nk, 8, rows), F32),
        vmem((nk, rows, rows), F32),
        vmem((rows, width), BF16),
        vmem((rows, width), BF16),
        vmem((rows, proj), BF16),
        vmem((rows, proj), BF16),
        vmem((m, PARTS * dk, rows), BF16),
        vmem((nk, PARTS * dk, rows), BF16),
        vmem((PARTS, rows, quarter), BF16),
        vmem((nk, rows, quarter), BF16),
        vmem((PARTS, dk, quarter), BF16),
        vmem((PARTS, dk, quarter), BF16),
        vmem((dk, quarter), BF16),
        vmem((PARTS, dk, quarter), BF16),
        pltpu.SemaphoreType.DMA((4,)),
    ]
    four, core, full = PARTS, 2 * m, nk
    for count in (four, four, full, full, core * PARTS, core, core, core, four, four, full, four, four):
        scratch += [pltpu.SemaphoreType.DMA((count,))] * 2
    macs = rows * proj * (2 * width + 2 * nk * rows) + PARTS * dk * nk * rows * quarter
    return pl.pallas_call(
        functools.partial(kernel, m),
        out_shape=(
            jax.ShapeDtypeStruct((rows, width), BF16),
            jax.ShapeDtypeStruct((dk, proj), F32),
        ),
        in_specs=[pl.BlockSpec(memory_space=pl.ANY)] * 4,
        out_specs=(pl.BlockSpec(memory_space=pltpu.VMEM), pl.BlockSpec(memory_space=pltpu.VMEM)),
        scratch_shapes=scratch,
        cost_estimate=pl.CostEstimate(flops=2 * macs, bytes_accessed=4 * rows * width + 2 * width * proj, transcendentals=rows * rows * nk),
        compiler_params=pltpu.CompilerParams(
            collective_id=0, has_side_effects=True, vmem_limit_bytes=60 * 1024 * 1024
        ),
    )(embeddings, labels.reshape(1, rows), order, head_weight)


def solution(mesh):
    m = mesh.shape["key"] // PARTS
    return jax.shard_map(
        functools.partial(body, m),
        mesh=mesh,
        in_specs=(P(("shuf", "key"), None), P(("shuf", "key")), P(("shuf", "key"), None), P()),
        out_specs=(P(("shuf", "key"), None), P("key", None)),
        check_vma=False,
    )
```

```python
import functools

import jax
import jax.numpy as jnp
from jax import lax
from jax.experimental import pallas as pl
from jax.experimental.pallas import tpu as pltpu
from jax.sharding import PartitionSpec as P

MESH = pl.DeviceIdType.MESH
F32, BF16 = jnp.float32, jnp.bfloat16
exponent_divisor = 0.1
loss_scale = 64.0
epsilon = 1e-06
PARTS = 4


def nn(a, b):
    return lax.dot_general(a, b, (((1,), (0,)), ((), ())), preferred_element_type=F32)


def nt(a, b):
    return lax.dot_general(a, b, (((1,), (1,)), ((), ())), preferred_element_type=F32)


def tn(a, b):
    return lax.dot_general(a, b, (((0,), (0,)), ((), ())), preferred_element_type=F32)


def kernel(
    m, emb_hbm, lab_hbm, order_hbm, head_hbm, gemb_ref, ghead_ref,
    emb_ref, lab_ref, order_ref, head_ref,
    slot_ref, group_ref, labs_ref, labz_ref, labg_ref, wts_ref, wtg_ref, exp_ref, coef_ref,
    embs_ref, embz_ref, slope_ref, slopez_ref, embt_ref, embg_ref, slq_ref, slg_ref,
    hs_ref, hz_ref, qs_ref, qg_ref,
    in_sem, zs_sem, zr_sem, lzs_sem, lzr_sem, lgs_sem, lgr_sem, wgs_sem, wgr_sem,
    gs_sem, gr_sem, gfs_sem, gfr_sem, es_sem, er_sem, efs_sem, efr_sem,
    ts_sem, tr_sem, cs_sem, cr_sem, ss_sem, sr_sem, hs_sem, hr_sem, qs_sem, qr_sem,
):
    rows, width = emb_ref.shape
    slab = rows // PARTS
    nk = PARTS * m
    dk = width // nk
    quarter = head_ref.shape[1] // PARTS
    u = lax.axis_index("shuf")
    k = lax.axis_index("key")
    z, j = k // m, k % m

    def flip(a, du):
        for bit in (1, 2):
            if du & bit:
                a = a + bit - 2 * bit * ((a // bit) % 2)
        return a

    def ahead(dz):
        return (z + dz) % PARTS

    def behind(dz):
        return (z + PARTS - dz) % PARTS

    def there(du, dj):
        return flip(u, du), (j + dj) % m

    def origin(du, dj):
        return flip(u, du), (j + m - dj) % m

    def block_of(uj):
        return uj[0] * m + uj[1]

    def block_rows(ref, b):
        return ref.at[pl.ds(pl.multiple_of(b * rows, rows), rows)]

    def lanes_of(b):
        return pl.ds(pl.multiple_of(b * rows, rows), rows)

    def u_rows(ref, uu):
        return ref[pl.ds(pl.multiple_of(uu * (m * rows), m * rows), m * rows), :]

    def emb_cols(b):
        return embg_ref.at[b // m, :, lanes_of(b % m)]

    def plane_id(uj):
        return (uj[0], z * m + uj[1])

    def z_id(zz):
        return (u, zz * m + j)

    pending = []

    def send(src, dst, s_sem, r_sem, to):
        copy = pltpu.make_async_remote_copy(
            src_ref=src, dst_ref=dst, send_sem=s_sem, recv_sem=r_sem, device_id=to, device_id_type=MESH
        )
        copy.start()
        pending.append(copy)

    def arrived(dst, s_sem, r_sem, frm):
        pltpu.make_async_remote_copy(
            src_ref=dst, dst_ref=dst, send_sem=s_sem, recv_sem=r_sem, device_id=frm, device_id_type=MESH
        ).wait_recv()

    def drain(copies):
        for copy in copies:
            copy.wait_send()

    same_core = [(du, dj) for dj in range(m) for du in (0, 2)]
    plane = [(du, dj) for dj in range(m) for du in range(PARTS)]
    mine = block_of((u, j))

    loads = [
        pltpu.make_async_copy(src, dst, in_sem.at[i])
        for i, (src, dst) in enumerate(
            [(order_hbm, order_ref), (emb_hbm, emb_ref), (lab_hbm, lab_ref), (head_hbm, head_ref)]
        )
    ]
    for load in loads:
        load.start()
    barrier = pltpu.get_barrier_semaphore()
    for off in plane[1:]:
        pl.semaphore_signal(barrier, inc=1, device_id=plane_id(there(*off)), device_id_type=MESH)
    for dz in range(1, PARTS):
        pl.semaphore_signal(barrier, inc=1, device_id=z_id(ahead(dz)), device_id_type=MESH)

    sub = lax.broadcasted_iota(jnp.int32, (rows, rows), 0)
    lane = lax.broadcasted_iota(jnp.int32, (rows, rows), 1)
    eye = sub == lane
    loads[0].wait()
    place = sub == order_ref[...]
    place_bf = place.astype(F32).astype(BF16)

    def directions(x):
        projected = nn(x, head_ref[...])
        row_norm = jnp.sqrt(jnp.sum(projected * projected, axis=1, keepdims=True) + epsilon)
        return projected / row_norm, row_norm

    loads[2].wait()
    loads[1].wait()
    loads[3].wait()
    slot_ref[...] = tn(place_bf, directions(emb_ref[...])[0].astype(BF16)).astype(BF16)

    def column(row):
        return jnp.sum(jnp.where(eye, row, 0.0), axis=1, keepdims=True)

    def row_of(col):
        return jnp.sum(jnp.where(eye, col, 0.0), axis=0, keepdims=True)

    lab_col = column(lab_ref[...].astype(F32))
    lab_slot = jnp.sum(jnp.where(place, lab_col, 0.0), axis=0, keepdims=True)
    labs_ref[...] = jnp.broadcast_to(lab_slot, labs_ref.shape)
    pl.semaphore_wait(barrier, nk - 1 + PARTS - 1)

    def slab_rows(ref, i):
        return ref.at[pl.ds(pl.multiple_of(i * slab, slab), slab)]

    def group_slab(b, i):
        return group_ref.at[pl.ds(pl.multiple_of(b * rows + i * slab, slab), slab)]

    for dz in range(1, PARTS):
        zz = ahead(dz)
        send(slab_rows(slot_ref, zz), group_slab(mine, z), zs_sem.at[dz], zr_sem.at[dz], z_id(zz))
    for dz in range(1, PARTS):
        send(labs_ref, labz_ref.at[z], lzs_sem.at[dz], lzr_sem.at[dz], z_id(ahead(dz)))
    own = pl.multiple_of(mine * rows + z * slab, slab)
    own_slot = pl.multiple_of(z * slab, slab)
    group_ref[pl.ds(own, slab), :] = slot_ref[pl.ds(own_slot, slab), :]
    labz_ref[z] = labs_ref[...]
    embs_ref[...] = tn(place_bf, emb_ref[...]).astype(BF16)

    def extract(buf_ref):
        lanes = lax.broadcasted_iota(jnp.int32, (8, rows), 1) // slab
        out = jnp.zeros((8, rows), F32)
        for i in range(PARTS):
            moved = pltpu.roll(buf_ref[i], ((i + PARTS - z) % PARTS) * slab, 1)
            out = jnp.where(lanes == i, moved, out)
        return out

    for dz in range(PARTS):
        piece = group_slab(mine, behind(dz))
        if dz:
            arrived(piece, zs_sem.at[dz], zr_sem.at[dz], z_id(behind(dz)))
        for i, off in enumerate(same_core):
            if i:
                n = i * PARTS + dz
                send(piece, piece, gs_sem.at[n], gr_sem.at[n], plane_id(there(*off)))
        if dz == PARTS - 2:
            embz_ref[pl.ds(own_slot, slab), :] = embs_ref[pl.ds(own_slot, slab), :]
            for step in range(1, PARTS):
                zz = ahead(step)
                send(slab_rows(embs_ref, zz), slab_rows(embz_ref, z), cs_sem.at[step], cr_sem.at[step], z_id(zz))
    partner = there(1, 0)
    send(block_rows(group_ref, mine), block_rows(group_ref, mine), gfs_sem.at[0], gfr_sem.at[0], plane_id(partner))
    for dz in range(1, PARTS):
        arrived(labz_ref.at[behind(dz)], lzs_sem.at[dz], lzr_sem.at[dz], z_id(behind(dz)))
    own_label = extract(labz_ref)
    labg_ref[:, lanes_of(mine)] = own_label
    for i, off in enumerate(plane):
        if i:
            send(labg_ref.at[:, lanes_of(mine)], labg_ref.at[:, lanes_of(mine)], lgs_sem.at[i], lgr_sem.at[i], plane_id(there(*off)))

    anchors = group_ref[pl.ds(pl.multiple_of(mine * rows, rows), rows), :]
    anchor_col = column(own_label[0:1, :])
    wide = m * rows
    row_id = lax.broadcasted_iota(jnp.int32, (rows, wide), 0) + mine * rows
    lane_id = lax.broadcasted_iota(jnp.int32, (rows, wide), 1)

    def exponent_of(uu, own):
        value = jnp.exp(nt(anchors, u_rows(group_ref, uu)) / exponent_divisor)
        if own:
            value = jnp.where(row_id == lane_id + uu * wide, 0.0, value)
        exp_ref[uu] = value
        return jnp.sum(value, axis=1, keepdims=True)

    def positive_of(uu):
        same = jnp.logical_and(
            anchor_col == labg_ref[0:1, uu * wide : (uu + 1) * wide], row_id != lane_id + uu * wide
        )
        return jnp.where(same, 1.0, 0.0)

    def gathered(du):
        for i, off in enumerate(same_core):
            if i and off[0] == du:
                frm = origin(*off)
                b = block_of(frm)
                for dz in range(PARTS):
                    n = i * PARTS + dz
                    arrived(group_slab(b, behind(dz)), gs_sem.at[n], gr_sem.at[n], plane_id(frm))
                send(block_rows(group_ref, b), block_rows(group_ref, b), gfs_sem.at[i], gfr_sem.at[i], plane_id(partner))

    def forwarded(du):
        for i, off in enumerate(same_core):
            if off[0] == du:
                uj = origin(*off)
                b = block_of((flip(uj[0], 1), uj[1]))
                yield i, b

    gathered(0)
    total = exponent_of(u, True)
    gathered(2)
    total = total + exponent_of(flip(u, 2), False)
    for i, off in enumerate(plane):
        if i:
            frm = origin(*off)
            arrived(labg_ref.at[:, lanes_of(block_of(frm))], lgs_sem.at[i], lgr_sem.at[i], plane_id(frm))
    counts = jnp.sum(positive_of(0), axis=1, keepdims=True)
    for uu in range(1, PARTS):
        counts = counts + jnp.sum(positive_of(uu), axis=1, keepdims=True)
    for du in (0, 2):
        for i, b in forwarded(du):
            arrived(block_rows(group_ref, b), gfs_sem.at[i], gfr_sem.at[i], plane_id(partner))
        total = total + exponent_of(flip(u, du + 1), False)
    totals = total
    floor_count = jnp.maximum(counts, 1.0)
    soft = loss_scale * counts / (floor_count * totals)
    pos = loss_scale / floor_count
    first_row = lax.broadcasted_iota(jnp.int32, (8, rows), 0) == 0
    wts_ref[...] = jnp.where(first_row, row_of(soft), row_of(pos))
    wtg_ref[:, lanes_of(mine)] = wts_ref[...]
    for i, off in enumerate(plane):
        if i:
            send(wts_ref, wtg_ref.at[:, lanes_of(mine)], wgs_sem.at[i], wgr_sem.at[i], plane_id(there(*off)))

    for dz in range(1, PARTS):
        arrived(slab_rows(embz_ref, behind(dz)), cs_sem.at[dz], cr_sem.at[dz], z_id(behind(dz)))
    turned = embz_ref[...].T
    for jj in range(m):
        for zz in range(PARTS):
            start = (zz * m + jj) * dk
            embt_ref[jj, zz * dk : (zz + 1) * dk, :] = turned[start : start + dk, :]
    for i, off in enumerate(same_core):
        if i:
            to = there(*off)
            send(embt_ref.at[to[1]], emb_cols(mine), es_sem.at[i], er_sem.at[i], plane_id(to))
    embg_ref[u, :, lanes_of(j)] = embt_ref[j]
    send(emb_cols(mine), emb_cols(mine), efs_sem.at[0], efr_sem.at[0], plane_id(partner))
    direction, row_norm = directions(embz_ref[...])

    for i, off in enumerate(plane):
        if i:
            frm = origin(*off)
            arrived(wtg_ref.at[:, lanes_of(block_of(frm))], wgs_sem.at[i], wgr_sem.at[i], plane_id(frm))
    for uu in range(PARTS):
        cols = slice(uu * wide, (uu + 1) * wide)
        coefficient = (soft + wtg_ref[0:1, cols]) * exp_ref[uu] - (pos + wtg_ref[1:2, cols]) * positive_of(uu)
        coef_ref[:, cols] = coefficient.astype(BF16)
    pull = nn(coef_ref[...], group_ref[...]) / exponent_divisor
    slopes = (pull - direction * jnp.sum(direction * pull, axis=1, keepdims=True)) / row_norm
    slopes = slopes.astype(BF16)
    slope_ref[...] = slopes
    for uu in range(PARTS):
        slq_ref[uu] = slopes[:, uu * quarter : (uu + 1) * quarter]
    for i, off in enumerate(plane):
        if i:
            to = there(*off)
            send(slq_ref.at[to[0]], block_rows(slg_ref, mine), ss_sem.at[i], sr_sem.at[i], plane_id(to))
    slg_ref[pl.ds(pl.multiple_of(mine * rows, rows), rows), :] = slq_ref[u]
    for dz in range(1, PARTS):
        zz = ahead(dz)
        send(slab_rows(slope_ref, zz), slab_rows(slopez_ref, z), ts_sem.at[dz], tr_sem.at[dz], z_id(zz))
    slopez_ref[pl.ds(own_slot, slab), :] = slope_ref[pl.ds(own_slot, slab), :]
    for i, off in enumerate(same_core):
        if i:
            frm = origin(*off)
            b = block_of(frm)
            arrived(emb_cols(b), es_sem.at[i], er_sem.at[i], plane_id(frm))
            send(emb_cols(b), emb_cols(b), efs_sem.at[i], efr_sem.at[i], plane_id(partner))
    part = None
    for du in range(PARTS):
        if du % 2:
            for i, b in forwarded(du - 1):
                arrived(emb_cols(b), efs_sem.at[i], efr_sem.at[i], plane_id(partner))
        for i, off in enumerate(plane):
            if i and off[0] == du:
                frm = origin(*off)
                arrived(block_rows(slg_ref, block_of(frm)), ss_sem.at[i], sr_sem.at[i], plane_id(frm))
        term = nn(embg_ref[flip(u, du)], u_rows(slg_ref, flip(u, du)))
        part = term if part is None else part + term
    earlier = len(pending)
    hs_ref[...] = part.astype(BF16).reshape(hs_ref.shape)
    for dz in range(1, PARTS):
        zz = ahead(dz)
        send(hs_ref.at[zz], hz_ref.at[z], hs_sem.at[dz], hr_sem.at[dz], z_id(zz))
    hz_ref[z] = hs_ref[z]
    for dz in range(1, PARTS):
        frm = behind(dz)
        arrived(slab_rows(slopez_ref, frm), ts_sem.at[dz], tr_sem.at[dz], z_id(frm))
    drain(pending[:earlier])
    gemb_ref[...] = nt(nn(place_bf, slopez_ref[...]).astype(BF16), head_ref[...]).astype(BF16)
    for dz in range(1, PARTS):
        arrived(hz_ref.at[behind(dz)], hs_sem.at[dz], hr_sem.at[dz], z_id(behind(dz)))
    part = hz_ref[0].astype(F32)
    for zz in range(1, PARTS):
        part = part + hz_ref[zz].astype(F32)
    qs_ref[...] = (part / loss_scale).astype(BF16)
    for du in range(1, PARTS):
        send(qs_ref, qg_ref.at[u], qs_sem.at[du], qr_sem.at[du], plane_id(there(du, 0)))
    qg_ref[u] = qs_ref[...]
    for du in range(1, PARTS):
        frm = origin(du, 0)
        arrived(qg_ref.at[frm[0]], qs_sem.at[du], qr_sem.at[du], plane_id(frm))
    for uu in range(PARTS):
        ghead_ref[:, uu * quarter : (uu + 1) * quarter] = qg_ref[uu].astype(F32)
    drain(pending[earlier:])


def body(m, embeddings, labels, order, head_weight):
    rows, width = embeddings.shape
    proj = head_weight.shape[1]
    nk = PARTS * m
    dk = width // nk
    quarter = proj // PARTS
    vmem = pltpu.VMEM
    scratch = [
        vmem((rows, width), BF16),
        vmem((1, rows), jnp.int32),
        vmem((1, rows), jnp.int32),
        vmem((width, proj), BF16),
        vmem((rows, proj), BF16),
        vmem((nk * rows, proj), BF16),
        vmem((8, rows), F32),
        vmem((PARTS, 8, rows), F32),
        vmem((8, nk * rows), F32),
        vmem((8, rows), F32),
        vmem((8, nk * rows), F32),
        vmem((PARTS, rows, m * rows), F32),
        vmem((rows, nk * rows), BF16),
        vmem((rows, width), BF16),
        vmem((rows, width), BF16),
        vmem((rows, proj), BF16),
        vmem((rows, proj), BF16),
        vmem((m, PARTS * dk, rows), BF16),
        vmem((PARTS, PARTS * dk, m * rows), BF16),
        vmem((PARTS, rows, quarter), BF16),
        vmem((nk * rows, quarter), BF16),
        vmem((PARTS, dk, quarter), BF16),
        vmem((PARTS, dk, quarter), BF16),
        vmem((dk, quarter), BF16),
        vmem((PARTS, dk, quarter), BF16),
        pltpu.SemaphoreType.DMA((4,)),
    ]
    four, core, full = PARTS, 2 * m, nk
    for count in (four, four, full, full, core * PARTS, core, core, core, four, four, full, four, four):
        scratch += [pltpu.SemaphoreType.DMA((count,))] * 2
    macs = rows * proj * (2 * width + 2 * nk * rows) + PARTS * dk * nk * rows * quarter
    return pl.pallas_call(
        functools.partial(kernel, m),
        out_shape=(
            jax.ShapeDtypeStruct((rows, width), BF16),
            jax.ShapeDtypeStruct((dk, proj), F32),
        ),
        in_specs=[pl.BlockSpec(memory_space=pltpu.HBM)] * 4,
        out_specs=(pl.BlockSpec(memory_space=pltpu.VMEM), pl.BlockSpec(memory_space=pltpu.VMEM)),
        scratch_shapes=scratch,
        cost_estimate=pl.CostEstimate(flops=2 * macs, bytes_accessed=4 * rows * width + 2 * width * proj, transcendentals=rows * rows * nk),
        compiler_params=pltpu.CompilerParams(
            collective_id=0, has_side_effects=True, vmem_limit_bytes=32 * 1024 * 1024
        ),
    )(embeddings, labels.reshape(1, rows), order, head_weight)


def solution(mesh):
    m = mesh.shape["key"] // PARTS
    return jax.shard_map(
        functools.partial(body, m),
        mesh=mesh,
        in_specs=(P(("shuf", "key"), None), P(("shuf", "key")), P(("shuf", "key"), None), P()),
        out_specs=(P(("shuf", "key"), None), P("key", None)),
        check_vma=False,
    )
```

```python
import functools

import jax
import jax.numpy as jnp
from jax import lax
from jax.experimental import pallas as pl
from jax.experimental.pallas import tpu as pltpu
from jax.sharding import PartitionSpec as P

MESH = pl.DeviceIdType.MESH
F32, BF16 = jnp.float32, jnp.bfloat16
exponent_divisor = 0.1
loss_scale = 64.0
epsilon = 1e-06
PARTS = 4


def nn(a, b):
    return lax.dot_general(a, b, (((1,), (0,)), ((), ())), preferred_element_type=F32)


def nt(a, b):
    return lax.dot_general(a, b, (((1,), (1,)), ((), ())), preferred_element_type=F32)


def tn(a, b):
    return lax.dot_general(a, b, (((0,), (0,)), ((), ())), preferred_element_type=F32)


def kernel(
    m, emb_hbm, lab_hbm, order_hbm, head_hbm, gemb_ref, ghead_ref,
    emb_ref, lab_ref, order_ref, head_ref,
    slot_ref, group_ref, labs_ref, labz_ref, labg_ref, wts_ref, wtg_ref, exp_ref, coef_ref,
    embs_ref, embz_ref, slope_ref, slopez_ref, embt_ref, embg_ref, slq_ref, slg_ref,
    hs_ref, hz_ref, qs_ref, qg_ref,
    in_sem, zs_sem, zr_sem, lzs_sem, lzr_sem, lgs_sem, lgr_sem, wgs_sem, wgr_sem,
    gs_sem, gr_sem, gfs_sem, gfr_sem, es_sem, er_sem, efs_sem, efr_sem,
    ts_sem, tr_sem, cs_sem, cr_sem, ss_sem, sr_sem, hs_sem, hr_sem, qs_sem, qr_sem,
):
    rows, width = emb_ref.shape
    slab = rows // PARTS
    nk = PARTS * m
    dk = width // nk
    quarter = head_ref.shape[1] // PARTS
    u = lax.axis_index("shuf")
    k = lax.axis_index("key")
    z, j = k // m, k % m

    def flip(a, du):
        for bit in (1, 2):
            if du & bit:
                a = a + bit - 2 * bit * ((a // bit) % 2)
        return a

    def ahead(dz):
        return (z + dz) % PARTS

    def behind(dz):
        return (z + PARTS - dz) % PARTS

    def there(du, dj):
        return flip(u, du), (j + dj) % m

    def origin(du, dj):
        return flip(u, du), (j + m - dj) % m

    def block_of(uj):
        return uj[0] * m + uj[1]

    def block_rows(ref, b):
        return ref.at[pl.ds(pl.multiple_of(b * rows, rows), rows)]

    def lanes_of(b):
        return pl.ds(pl.multiple_of(b * rows, rows), rows)

    def u_rows(ref, uu):
        return ref[pl.ds(pl.multiple_of(uu * (m * rows), m * rows), m * rows), :]

    def emb_cols(b):
        return embg_ref.at[b // m, :, lanes_of(b % m)]

    def plane_id(uj):
        return (uj[0], z * m + uj[1])

    def z_id(zz):
        return (u, zz * m + j)

    pending = []

    def send(src, dst, s_sem, r_sem, to):
        copy = pltpu.make_async_remote_copy(
            src_ref=src, dst_ref=dst, send_sem=s_sem, recv_sem=r_sem, device_id=to, device_id_type=MESH
        )
        copy.start()
        pending.append(copy)

    def arrived(dst, s_sem, r_sem, frm):
        pltpu.make_async_remote_copy(
            src_ref=dst, dst_ref=dst, send_sem=s_sem, recv_sem=r_sem, device_id=frm, device_id_type=MESH
        ).wait_recv()

    def drain(copies):
        for copy in copies:
            copy.wait_send()

    same_core = [(du, dj) for dj in range(m) for du in (0, 2)]
    plane = [(du, dj) for dj in range(m) for du in range(PARTS)]
    mine = block_of((u, j))

    loads = [
        pltpu.make_async_copy(src, dst, in_sem.at[i])
        for i, (src, dst) in enumerate(
            [(order_hbm, order_ref), (emb_hbm, emb_ref), (lab_hbm, lab_ref), (head_hbm, head_ref)]
        )
    ]
    for load in loads:
        load.start()
    barrier = pltpu.get_barrier_semaphore()
    for off in plane[1:]:
        pl.semaphore_signal(barrier, inc=1, device_id=plane_id(there(*off)), device_id_type=MESH)
    for dz in range(1, PARTS):
        pl.semaphore_signal(barrier, inc=1, device_id=z_id(ahead(dz)), device_id_type=MESH)

    sub = lax.broadcasted_iota(jnp.int32, (rows, rows), 0)
    lane = lax.broadcasted_iota(jnp.int32, (rows, rows), 1)
    eye = sub == lane
    loads[0].wait()
    place = sub == order_ref[...]
    place_bf = place.astype(F32).astype(BF16)

    def directions(x):
        projected = nn(x, head_ref[...])
        row_norm = jnp.sqrt(jnp.sum(projected * projected, axis=1, keepdims=True) + epsilon)
        return projected / row_norm, row_norm

    loads[2].wait()
    loads[1].wait()
    loads[3].wait()
    slot_ref[...] = tn(place_bf, directions(emb_ref[...])[0].astype(BF16)).astype(BF16)

    def column(row):
        return jnp.sum(jnp.where(eye, row, 0.0), axis=1, keepdims=True)

    def row_of(col):
        return jnp.sum(jnp.where(eye, col, 0.0), axis=0, keepdims=True)

    lab_col = column(lab_ref[...].astype(F32))
    lab_slot = jnp.sum(jnp.where(place, lab_col, 0.0), axis=0, keepdims=True)
    labs_ref[...] = jnp.broadcast_to(lab_slot, labs_ref.shape)
    pl.semaphore_wait(barrier, nk - 1 + PARTS - 1)

    def slab_rows(ref, i):
        return ref.at[pl.ds(pl.multiple_of(i * slab, slab), slab)]

    def group_slab(b, i):
        return group_ref.at[pl.ds(pl.multiple_of(b * rows + i * slab, slab), slab)]

    for dz in range(1, PARTS):
        zz = ahead(dz)
        send(slab_rows(slot_ref, zz), group_slab(mine, z), zs_sem.at[dz], zr_sem.at[dz], z_id(zz))
    for dz in range(1, PARTS):
        send(labs_ref, labz_ref.at[z], lzs_sem.at[dz], lzr_sem.at[dz], z_id(ahead(dz)))
    own = pl.multiple_of(mine * rows + z * slab, slab)
    own_slot = pl.multiple_of(z * slab, slab)
    group_ref[pl.ds(own, slab), :] = slot_ref[pl.ds(own_slot, slab), :]
    labz_ref[z] = labs_ref[...]
    embs_ref[...] = tn(place_bf, emb_ref[...]).astype(BF16)
    embz_ref[pl.ds(own_slot, slab), :] = embs_ref[pl.ds(own_slot, slab), :]
    for dz in range(1, PARTS):
        zz = ahead(dz)
        send(slab_rows(embs_ref, zz), slab_rows(embz_ref, z), cs_sem.at[dz], cr_sem.at[dz], z_id(zz))

    def extract(buf_ref):
        lanes = lax.broadcasted_iota(jnp.int32, (8, rows), 1) // slab
        out = jnp.zeros((8, rows), F32)
        for i in range(PARTS):
            moved = pltpu.roll(buf_ref[i], ((i + PARTS - z) % PARTS) * slab, 1)
            out = jnp.where(lanes == i, moved, out)
        return out

    for dz in range(PARTS):
        piece = group_slab(mine, behind(dz))
        if dz:
            arrived(piece, zs_sem.at[dz], zr_sem.at[dz], z_id(behind(dz)))
        for i, off in enumerate(same_core):
            if i:
                n = i * PARTS + dz
                send(piece, piece, gs_sem.at[n], gr_sem.at[n], plane_id(there(*off)))
    partner = there(1, 0)
    send(block_rows(group_ref, mine), block_rows(group_ref, mine), gfs_sem.at[0], gfr_sem.at[0], plane_id(partner))
    for dz in range(1, PARTS):
        arrived(labz_ref.at[behind(dz)], lzs_sem.at[dz], lzr_sem.at[dz], z_id(behind(dz)))
    own_label = extract(labz_ref)
    labg_ref[:, lanes_of(mine)] = own_label
    for i, off in enumerate(plane):
        if i:
            send(labg_ref.at[:, lanes_of(mine)], labg_ref.at[:, lanes_of(mine)], lgs_sem.at[i], lgr_sem.at[i], plane_id(there(*off)))

    anchors = group_ref[pl.ds(pl.multiple_of(mine * rows, rows), rows), :]
    anchor_col = column(own_label[0:1, :])
    wide = m * rows
    row_id = lax.broadcasted_iota(jnp.int32, (rows, wide), 0) + mine * rows
    lane_id = lax.broadcasted_iota(jnp.int32, (rows, wide), 1)

    def exponent_of(uu, own):
        value = jnp.exp(nt(anchors, u_rows(group_ref, uu)) / exponent_divisor)
        if own:
            value = jnp.where(row_id == lane_id + uu * wide, 0.0, value)
        exp_ref[uu] = value
        return jnp.sum(value, axis=1, keepdims=True)

    def positive_of(uu):
        same = jnp.logical_and(
            anchor_col == labg_ref[0:1, uu * wide : (uu + 1) * wide], row_id != lane_id + uu * wide
        )
        return jnp.where(same, 1.0, 0.0)

    def gathered(du):
        for i, off in enumerate(same_core):
            if i and off[0] == du:
                frm = origin(*off)
                b = block_of(frm)
                for dz in range(PARTS):
                    n = i * PARTS + dz
                    arrived(group_slab(b, behind(dz)), gs_sem.at[n], gr_sem.at[n], plane_id(frm))
                send(block_rows(group_ref, b), block_rows(group_ref, b), gfs_sem.at[i], gfr_sem.at[i], plane_id(partner))

    def forwarded(du):
        for i, off in enumerate(same_core):
            if off[0] == du:
                uj = origin(*off)
                b = block_of((flip(uj[0], 1), uj[1]))
                yield i, b

    gathered(0)
    total = exponent_of(u, True)
    gathered(2)
    total = total + exponent_of(flip(u, 2), False)
    for i, off in enumerate(plane):
        if i:
            frm = origin(*off)
            arrived(labg_ref.at[:, lanes_of(block_of(frm))], lgs_sem.at[i], lgr_sem.at[i], plane_id(frm))
    counts = jnp.sum(positive_of(0), axis=1, keepdims=True)
    for uu in range(1, PARTS):
        counts = counts + jnp.sum(positive_of(uu), axis=1, keepdims=True)
    for du in (0, 2):
        for i, b in forwarded(du):
            arrived(block_rows(group_ref, b), gfs_sem.at[i], gfr_sem.at[i], plane_id(partner))
        total = total + exponent_of(flip(u, du + 1), False)
    totals = total
    floor_count = jnp.maximum(counts, 1.0)
    soft = loss_scale * counts / (floor_count * totals)
    pos = loss_scale / floor_count
    first_row = lax.broadcasted_iota(jnp.int32, (8, rows), 0) == 0
    wts_ref[...] = jnp.where(first_row, row_of(soft), row_of(pos))
    wtg_ref[:, lanes_of(mine)] = wts_ref[...]
    for i, off in enumerate(plane):
        if i:
            send(wts_ref, wtg_ref.at[:, lanes_of(mine)], wgs_sem.at[i], wgr_sem.at[i], plane_id(there(*off)))

    for dz in range(1, PARTS):
        arrived(slab_rows(embz_ref, behind(dz)), cs_sem.at[dz], cr_sem.at[dz], z_id(behind(dz)))
    turned = embz_ref[...].T
    for jj in range(m):
        for zz in range(PARTS):
            start = (zz * m + jj) * dk
            embt_ref[jj, zz * dk : (zz + 1) * dk, :] = turned[start : start + dk, :]
    for i, off in enumerate(same_core):
        if i:
            to = there(*off)
            send(embt_ref.at[to[1]], emb_cols(mine), es_sem.at[i], er_sem.at[i], plane_id(to))
    embg_ref[u, :, lanes_of(j)] = embt_ref[j]
    send(emb_cols(mine), emb_cols(mine), efs_sem.at[0], efr_sem.at[0], plane_id(partner))
    direction, row_norm = directions(embz_ref[...])

    for i, off in enumerate(plane):
        if i:
            frm = origin(*off)
            arrived(wtg_ref.at[:, lanes_of(block_of(frm))], wgs_sem.at[i], wgr_sem.at[i], plane_id(frm))
    for uu in range(PARTS):
        cols = slice(uu * wide, (uu + 1) * wide)
        coefficient = (soft + wtg_ref[0:1, cols]) * exp_ref[uu] - (pos + wtg_ref[1:2, cols]) * positive_of(uu)
        coef_ref[:, cols] = coefficient.astype(BF16)
    pull = nn(coef_ref[...], group_ref[...]) / exponent_divisor
    slopes = (pull - direction * jnp.sum(direction * pull, axis=1, keepdims=True)) / row_norm
    slopes = slopes.astype(BF16)
    slope_ref[...] = slopes
    for uu in range(PARTS):
        slq_ref[uu] = slopes[:, uu * quarter : (uu + 1) * quarter]
    for i, off in enumerate(plane):
        if i:
            to = there(*off)
            send(slq_ref.at[to[0]], block_rows(slg_ref, mine), ss_sem.at[i], sr_sem.at[i], plane_id(to))
    slg_ref[pl.ds(pl.multiple_of(mine * rows, rows), rows), :] = slq_ref[u]
    for dz in range(1, PARTS):
        zz = ahead(dz)
        send(slab_rows(slope_ref, zz), slab_rows(slopez_ref, z), ts_sem.at[dz], tr_sem.at[dz], z_id(zz))
    slopez_ref[pl.ds(own_slot, slab), :] = slope_ref[pl.ds(own_slot, slab), :]
    for i, off in enumerate(same_core):
        if i:
            frm = origin(*off)
            b = block_of(frm)
            arrived(emb_cols(b), es_sem.at[i], er_sem.at[i], plane_id(frm))
            send(emb_cols(b), emb_cols(b), efs_sem.at[i], efr_sem.at[i], plane_id(partner))
    part = None
    for du in range(PARTS):
        if du % 2:
            for i, b in forwarded(du - 1):
                arrived(emb_cols(b), efs_sem.at[i], efr_sem.at[i], plane_id(partner))
        for i, off in enumerate(plane):
            if i and off[0] == du:
                frm = origin(*off)
                arrived(block_rows(slg_ref, block_of(frm)), ss_sem.at[i], sr_sem.at[i], plane_id(frm))
        term = nn(embg_ref[flip(u, du)], u_rows(slg_ref, flip(u, du)))
        part = term if part is None else part + term
    earlier = len(pending)
    hs_ref[...] = part.astype(BF16).reshape(hs_ref.shape)
    for dz in range(1, PARTS):
        zz = ahead(dz)
        send(hs_ref.at[zz], hz_ref.at[z], hs_sem.at[dz], hr_sem.at[dz], z_id(zz))
    hz_ref[z] = hs_ref[z]
    for dz in range(1, PARTS):
        frm = behind(dz)
        arrived(slab_rows(slopez_ref, frm), ts_sem.at[dz], tr_sem.at[dz], z_id(frm))
    drain(pending[:earlier])
    gemb_ref[...] = nt(nn(place_bf, slopez_ref[...]).astype(BF16), head_ref[...]).astype(BF16)
    for dz in range(1, PARTS):
        arrived(hz_ref.at[behind(dz)], hs_sem.at[dz], hr_sem.at[dz], z_id(behind(dz)))
    part = hz_ref[0].astype(F32)
    for zz in range(1, PARTS):
        part = part + hz_ref[zz].astype(F32)
    qs_ref[...] = (part / loss_scale).astype(BF16)
    for du in range(1, PARTS):
        send(qs_ref, qg_ref.at[u], qs_sem.at[du], qr_sem.at[du], plane_id(there(du, 0)))
    qg_ref[u] = qs_ref[...]
    for du in range(1, PARTS):
        frm = origin(du, 0)
        arrived(qg_ref.at[frm[0]], qs_sem.at[du], qr_sem.at[du], plane_id(frm))
    for uu in range(PARTS):
        ghead_ref[:, uu * quarter : (uu + 1) * quarter] = qg_ref[uu].astype(F32)
    drain(pending[earlier:])


def body(m, embeddings, labels, order, head_weight):
    rows, width = embeddings.shape
    proj = head_weight.shape[1]
    nk = PARTS * m
    dk = width // nk
    quarter = proj // PARTS
    vmem = pltpu.VMEM
    scratch = [
        vmem((rows, width), BF16),
        vmem((1, rows), jnp.int32),
        vmem((1, rows), jnp.int32),
        vmem((width, proj), BF16),
        vmem((rows, proj), BF16),
        vmem((nk * rows, proj), BF16),
        vmem((8, rows), F32),
        vmem((PARTS, 8, rows), F32),
        vmem((8, nk * rows), F32),
        vmem((8, rows), F32),
        vmem((8, nk * rows), F32),
        vmem((PARTS, rows, m * rows), F32),
        vmem((rows, nk * rows), BF16),
        vmem((rows, width), BF16),
        vmem((rows, width), BF16),
        vmem((rows, proj), BF16),
        vmem((rows, proj), BF16),
        vmem((m, PARTS * dk, rows), BF16),
        vmem((PARTS, PARTS * dk, m * rows), BF16),
        vmem((PARTS, rows, quarter), BF16),
        vmem((nk * rows, quarter), BF16),
        vmem((PARTS, dk, quarter), BF16),
        vmem((PARTS, dk, quarter), BF16),
        vmem((dk, quarter), BF16),
        vmem((PARTS, dk, quarter), BF16),
        pltpu.SemaphoreType.DMA((4,)),
    ]
    four, core, full = PARTS, 2 * m, nk
    for count in (four, four, full, full, core * PARTS, core, core, core, four, four, full, four, four):
        scratch += [pltpu.SemaphoreType.DMA((count,))] * 2
    macs = rows * proj * (2 * width + 2 * nk * rows) + PARTS * dk * nk * rows * quarter
    return pl.pallas_call(
        functools.partial(kernel, m),
        out_shape=(
            jax.ShapeDtypeStruct((rows, width), BF16),
            jax.ShapeDtypeStruct((dk, proj), F32),
        ),
        in_specs=[pl.BlockSpec(memory_space=pltpu.HBM)] * 4,
        out_specs=(pl.BlockSpec(memory_space=pltpu.VMEM), pl.BlockSpec(memory_space=pltpu.VMEM)),
        scratch_shapes=scratch,
        cost_estimate=pl.CostEstimate(flops=2 * macs, bytes_accessed=4 * rows * width + 2 * width * proj, transcendentals=rows * rows * nk),
        compiler_params=pltpu.CompilerParams(
            collective_id=0, has_side_effects=True, vmem_limit_bytes=60 * 1024 * 1024
        ),
    )(embeddings, labels.reshape(1, rows), order, head_weight)


def solution(mesh):
    m = mesh.shape["key"] // PARTS
    return jax.shard_map(
        functools.partial(body, m),
        mesh=mesh,
        in_specs=(P(("shuf", "key"), None), P(("shuf", "key")), P(("shuf", "key"), None), P()),
        out_specs=(P(("shuf", "key"), None), P("key", None)),
        check_vma=False,
    )
```

```python
import functools

import jax
import jax.numpy as jnp
from jax import lax
from jax.experimental import pallas as pl
from jax.experimental.pallas import tpu as pltpu
from jax.sharding import PartitionSpec as P

MESH = pl.DeviceIdType.MESH
F32, BF16 = jnp.float32, jnp.bfloat16
exponent_divisor = 0.1
loss_scale = 64.0
epsilon = 1e-06
PARTS = 4


def nn(a, b):
    return lax.dot_general(a, b, (((1,), (0,)), ((), ())), preferred_element_type=F32)


def nt(a, b):
    return lax.dot_general(a, b, (((1,), (1,)), ((), ())), preferred_element_type=F32)


def tn(a, b):
    return lax.dot_general(a, b, (((0,), (0,)), ((), ())), preferred_element_type=F32)


def kernel(
    m, emb_hbm, lab_hbm, order_hbm, head_hbm, gemb_ref, ghead_ref,
    emb_ref, lab_ref, order_ref, head_ref,
    slot_ref, group_ref, labs_ref, labz_ref, labg_ref, wts_ref, wtg_ref, exp_ref, coef_ref,
    embs_ref, embz_ref, slope_ref, slopez_ref, embt_ref, embg_ref, slq_ref, slg_ref,
    hs_ref, hz_ref, qs_ref, qg_ref,
    in_sem, zs_sem, zr_sem, lzs_sem, lzr_sem, lgs_sem, lgr_sem, wgs_sem, wgr_sem,
    gs_sem, gr_sem, gfs_sem, gfr_sem, es_sem, er_sem, efs_sem, efr_sem,
    ts_sem, tr_sem, cs_sem, cr_sem, ss_sem, sr_sem, hs_sem, hr_sem, qs_sem, qr_sem,
):
    rows, width = emb_ref.shape
    slab = rows // PARTS
    nk = PARTS * m
    dk = width // nk
    quarter = head_ref.shape[1] // PARTS
    u = lax.axis_index("shuf")
    k = lax.axis_index("key")
    z, j = k // m, k % m

    def flip(a, du):
        for bit in (1, 2):
            if du & bit:
                a = a + bit - 2 * bit * ((a // bit) % 2)
        return a

    def ahead(dz):
        return (z + dz) % PARTS

    def behind(dz):
        return (z + PARTS - dz) % PARTS

    def there(du, dj):
        return flip(u, du), (j + dj) % m

    def origin(du, dj):
        return flip(u, du), (j + m - dj) % m

    def block_of(uj):
        return uj[0] * m + uj[1]

    def block_rows(ref, b):
        return ref.at[pl.ds(pl.multiple_of(b * rows, rows), rows)]

    def lanes_of(b):
        return pl.ds(pl.multiple_of(b * rows, rows), rows)

    def u_rows(ref, uu):
        return ref[pl.ds(pl.multiple_of(uu * (m * rows), m * rows), m * rows), :]

    def emb_cols(b):
        return embg_ref.at[b // m, :, lanes_of(b % m)]

    def plane_id(uj):
        return (uj[0], z * m + uj[1])

    def z_id(zz):
        return (u, zz * m + j)

    pending = []

    def send(src, dst, s_sem, r_sem, to):
        copy = pltpu.make_async_remote_copy(
            src_ref=src, dst_ref=dst, send_sem=s_sem, recv_sem=r_sem, device_id=to, device_id_type=MESH
        )
        copy.start()
        pending.append(copy)

    def arrived(dst, s_sem, r_sem, frm):
        pltpu.make_async_remote_copy(
            src_ref=dst, dst_ref=dst, send_sem=s_sem, recv_sem=r_sem, device_id=frm, device_id_type=MESH
        ).wait_recv()

    def drain(copies):
        for copy in copies:
            copy.wait_send()

    same_core = [(du, dj) for dj in range(m) for du in (0, 2)]
    plane = [(du, dj) for dj in range(m) for du in range(PARTS)]
    mine = block_of((u, j))

    loads = [
        pltpu.make_async_copy(src, dst, in_sem.at[i])
        for i, (src, dst) in enumerate(
            [(order_hbm, order_ref), (emb_hbm, emb_ref), (lab_hbm, lab_ref), (head_hbm, head_ref)]
        )
    ]
    for load in loads:
        load.start()
    barrier = pltpu.get_barrier_semaphore()
    for off in plane[1:]:
        pl.semaphore_signal(barrier, inc=1, device_id=plane_id(there(*off)), device_id_type=MESH)
    for dz in range(1, PARTS):
        pl.semaphore_signal(barrier, inc=1, device_id=z_id(ahead(dz)), device_id_type=MESH)

    sub = lax.broadcasted_iota(jnp.int32, (rows, rows), 0)
    lane = lax.broadcasted_iota(jnp.int32, (rows, rows), 1)
    eye = sub == lane
    loads[0].wait()
    place = sub == order_ref[...]
    place_bf = place.astype(F32).astype(BF16)

    def directions(x):
        projected = nn(x, head_ref[...])
        row_norm = jnp.sqrt(jnp.sum(projected * projected, axis=1, keepdims=True) + epsilon)
        return projected / row_norm, row_norm

    loads[2].wait()
    loads[1].wait()
    loads[3].wait()
    slot_ref[...] = tn(place_bf, directions(emb_ref[...])[0].astype(BF16)).astype(BF16)

    def column(row):
        return jnp.sum(jnp.where(eye, row, 0.0), axis=1, keepdims=True)

    def row_of(col):
        return jnp.sum(jnp.where(eye, col, 0.0), axis=0, keepdims=True)

    lab_col = column(lab_ref[...].astype(F32))
    lab_slot = jnp.sum(jnp.where(place, lab_col, 0.0), axis=0, keepdims=True)
    labs_ref[...] = jnp.broadcast_to(lab_slot, labs_ref.shape)
    pl.semaphore_wait(barrier, nk - 1 + PARTS - 1)

    def slab_rows(ref, i):
        return ref.at[pl.ds(pl.multiple_of(i * slab, slab), slab)]

    def group_slab(b, i):
        return group_ref.at[pl.ds(pl.multiple_of(b * rows + i * slab, slab), slab)]

    for dz in range(1, PARTS):
        zz = ahead(dz)
        send(slab_rows(slot_ref, zz), group_slab(mine, z), zs_sem.at[dz], zr_sem.at[dz], z_id(zz))
    for dz in range(1, PARTS):
        send(labs_ref, labz_ref.at[z], lzs_sem.at[dz], lzr_sem.at[dz], z_id(ahead(dz)))
    own = pl.multiple_of(mine * rows + z * slab, slab)
    own_slot = pl.multiple_of(z * slab, slab)
    group_ref[pl.ds(own, slab), :] = slot_ref[pl.ds(own_slot, slab), :]
    labz_ref[z] = labs_ref[...]

    def extract(buf_ref):
        lanes = lax.broadcasted_iota(jnp.int32, (8, rows), 1) // slab
        out = jnp.zeros((8, rows), F32)
        for i in range(PARTS):
            moved = pltpu.roll(buf_ref[i], ((i + PARTS - z) % PARTS) * slab, 1)
            out = jnp.where(lanes == i, moved, out)
        return out

    for dz in range(PARTS):
        piece = group_slab(mine, behind(dz))
        if dz:
            arrived(piece, zs_sem.at[dz], zr_sem.at[dz], z_id(behind(dz)))
        for i, off in enumerate(same_core):
            if i:
                n = i * PARTS + dz
                send(piece, piece, gs_sem.at[n], gr_sem.at[n], plane_id(there(*off)))
        if dz == 0:
            embs_ref[...] = tn(place_bf, emb_ref[...]).astype(BF16)
            embz_ref[pl.ds(own_slot, slab), :] = embs_ref[pl.ds(own_slot, slab), :]
    for dz in range(1, PARTS):
        zz = ahead(dz)
        send(slab_rows(embs_ref, zz), slab_rows(embz_ref, z), cs_sem.at[dz], cr_sem.at[dz], z_id(zz))
    partner = there(1, 0)
    send(block_rows(group_ref, mine), block_rows(group_ref, mine), gfs_sem.at[0], gfr_sem.at[0], plane_id(partner))
    for dz in range(1, PARTS):
        arrived(labz_ref.at[behind(dz)], lzs_sem.at[dz], lzr_sem.at[dz], z_id(behind(dz)))
    own_label = extract(labz_ref)
    labg_ref[:, lanes_of(mine)] = own_label
    for i, off in enumerate(plane):
        if i:
            send(labg_ref.at[:, lanes_of(mine)], labg_ref.at[:, lanes_of(mine)], lgs_sem.at[i], lgr_sem.at[i], plane_id(there(*off)))

    anchors = group_ref[pl.ds(pl.multiple_of(mine * rows, rows), rows), :]
    anchor_col = column(own_label[0:1, :])
    wide = m * rows
    row_id = lax.broadcasted_iota(jnp.int32, (rows, wide), 0) + mine * rows
    lane_id = lax.broadcasted_iota(jnp.int32, (rows, wide), 1)

    def exponent_of(uu, own):
        value = jnp.exp(nt(anchors, u_rows(group_ref, uu)) / exponent_divisor)
        if own:
            value = jnp.where(row_id == lane_id + uu * wide, 0.0, value)
        exp_ref[uu] = value
        return jnp.sum(value, axis=1, keepdims=True)

    def positive_of(uu):
        same = jnp.logical_and(
            anchor_col == labg_ref[0:1, uu * wide : (uu + 1) * wide], row_id != lane_id + uu * wide
        )
        return jnp.where(same, 1.0, 0.0)

    def gathered(du):
        for i, off in enumerate(same_core):
            if i and off[0] == du:
                frm = origin(*off)
                b = block_of(frm)
                for dz in range(PARTS):
                    n = i * PARTS + dz
                    arrived(group_slab(b, behind(dz)), gs_sem.at[n], gr_sem.at[n], plane_id(frm))
                send(block_rows(group_ref, b), block_rows(group_ref, b), gfs_sem.at[i], gfr_sem.at[i], plane_id(partner))

    def forwarded(du):
        for i, off in enumerate(same_core):
            if off[0] == du:
                uj = origin(*off)
                b = block_of((flip(uj[0], 1), uj[1]))
                yield i, b

    gathered(0)
    gathered(2)
    total = exponent_of(u, True)
    total = total + exponent_of(flip(u, 2), False)
    for i, off in enumerate(plane):
        if i:
            frm = origin(*off)
            arrived(labg_ref.at[:, lanes_of(block_of(frm))], lgs_sem.at[i], lgr_sem.at[i], plane_id(frm))
    counts = jnp.sum(positive_of(0), axis=1, keepdims=True)
    for uu in range(1, PARTS):
        counts = counts + jnp.sum(positive_of(uu), axis=1, keepdims=True)
    for du in (0, 2):
        for i, b in forwarded(du):
            arrived(block_rows(group_ref, b), gfs_sem.at[i], gfr_sem.at[i], plane_id(partner))
        total = total + exponent_of(flip(u, du + 1), False)
    totals = total
    floor_count = jnp.maximum(counts, 1.0)
    soft = loss_scale * counts / (floor_count * totals)
    pos = loss_scale / floor_count
    first_row = lax.broadcasted_iota(jnp.int32, (8, rows), 0) == 0
    wts_ref[...] = jnp.where(first_row, row_of(soft), row_of(pos))
    wtg_ref[:, lanes_of(mine)] = wts_ref[...]
    for i, off in enumerate(plane):
        if i:
            send(wts_ref, wtg_ref.at[:, lanes_of(mine)], wgs_sem.at[i], wgr_sem.at[i], plane_id(there(*off)))

    for dz in range(1, PARTS):
        arrived(slab_rows(embz_ref, behind(dz)), cs_sem.at[dz], cr_sem.at[dz], z_id(behind(dz)))
    turned = embz_ref[...].T
    for jj in range(m):
        for zz in range(PARTS):
            start = (zz * m + jj) * dk
            embt_ref[jj, zz * dk : (zz + 1) * dk, :] = turned[start : start + dk, :]
    for i, off in enumerate(same_core):
        if i:
            to = there(*off)
            send(embt_ref.at[to[1]], emb_cols(mine), es_sem.at[i], er_sem.at[i], plane_id(to))
    embg_ref[u, :, lanes_of(j)] = embt_ref[j]
    send(emb_cols(mine), emb_cols(mine), efs_sem.at[0], efr_sem.at[0], plane_id(partner))
    direction, row_norm = directions(embz_ref[...])

    for i, off in enumerate(plane):
        if i:
            frm = origin(*off)
            arrived(wtg_ref.at[:, lanes_of(block_of(frm))], wgs_sem.at[i], wgr_sem.at[i], plane_id(frm))
    for uu in range(PARTS):
        cols = slice(uu * wide, (uu + 1) * wide)
        coefficient = (soft + wtg_ref[0:1, cols]) * exp_ref[uu] - (pos + wtg_ref[1:2, cols]) * positive_of(uu)
        coef_ref[:, cols] = coefficient.astype(BF16)
    pull = nn(coef_ref[...], group_ref[...]) / exponent_divisor
    slopes = (pull - direction * jnp.sum(direction * pull, axis=1, keepdims=True)) / row_norm
    slopes = slopes.astype(BF16)
    slope_ref[...] = slopes
    for uu in range(PARTS):
        slq_ref[uu] = slopes[:, uu * quarter : (uu + 1) * quarter]
    for i, off in enumerate(plane):
        if i:
            to = there(*off)
            send(slq_ref.at[to[0]], block_rows(slg_ref, mine), ss_sem.at[i], sr_sem.at[i], plane_id(to))
    slg_ref[pl.ds(pl.multiple_of(mine * rows, rows), rows), :] = slq_ref[u]
    for dz in range(1, PARTS):
        zz = ahead(dz)
        send(slab_rows(slope_ref, zz), slab_rows(slopez_ref, z), ts_sem.at[dz], tr_sem.at[dz], z_id(zz))
    slopez_ref[pl.ds(own_slot, slab), :] = slope_ref[pl.ds(own_slot, slab), :]
    for i, off in enumerate(same_core):
        if i:
            frm = origin(*off)
            b = block_of(frm)
            arrived(emb_cols(b), es_sem.at[i], er_sem.at[i], plane_id(frm))
            send(emb_cols(b), emb_cols(b), efs_sem.at[i], efr_sem.at[i], plane_id(partner))
    part = None
    for du in range(PARTS):
        if du % 2:
            for i, b in forwarded(du - 1):
                arrived(emb_cols(b), efs_sem.at[i], efr_sem.at[i], plane_id(partner))
        for i, off in enumerate(plane):
            if i and off[0] == du:
                frm = origin(*off)
                arrived(block_rows(slg_ref, block_of(frm)), ss_sem.at[i], sr_sem.at[i], plane_id(frm))
        term = nn(embg_ref[flip(u, du)], u_rows(slg_ref, flip(u, du)))
        part = term if part is None else part + term
    earlier = len(pending)
    hs_ref[...] = part.astype(BF16).reshape(hs_ref.shape)
    for dz in range(1, PARTS):
        zz = ahead(dz)
        send(hs_ref.at[zz], hz_ref.at[z], hs_sem.at[dz], hr_sem.at[dz], z_id(zz))
    hz_ref[z] = hs_ref[z]
    for dz in range(1, PARTS):
        frm = behind(dz)
        arrived(slab_rows(slopez_ref, frm), ts_sem.at[dz], tr_sem.at[dz], z_id(frm))
    drain(pending[:earlier])
    gemb_ref[...] = nt(nn(place_bf, slopez_ref[...]).astype(BF16), head_ref[...]).astype(BF16)
    for dz in range(1, PARTS):
        arrived(hz_ref.at[behind(dz)], hs_sem.at[dz], hr_sem.at[dz], z_id(behind(dz)))
    part = hz_ref[0].astype(F32)
    for zz in range(1, PARTS):
        part = part + hz_ref[zz].astype(F32)
    qs_ref[...] = (part / loss_scale).astype(BF16)
    for du in range(1, PARTS):
        send(qs_ref, qg_ref.at[u], qs_sem.at[du], qr_sem.at[du], plane_id(there(du, 0)))
    qg_ref[u] = qs_ref[...]
    for du in range(1, PARTS):
        frm = origin(du, 0)
        arrived(qg_ref.at[frm[0]], qs_sem.at[du], qr_sem.at[du], plane_id(frm))
    for uu in range(PARTS):
        ghead_ref[:, uu * quarter : (uu + 1) * quarter] = qg_ref[uu].astype(F32)
    drain(pending[earlier:])


def body(m, embeddings, labels, order, head_weight):
    rows, width = embeddings.shape
    proj = head_weight.shape[1]
    nk = PARTS * m
    dk = width // nk
    quarter = proj // PARTS
    vmem = pltpu.VMEM
    scratch = [
        vmem((rows, width), BF16),
        vmem((1, rows), jnp.int32),
        vmem((1, rows), jnp.int32),
        vmem((width, proj), BF16),
        vmem((rows, proj), BF16),
        vmem((nk * rows, proj), BF16),
        vmem((8, rows), F32),
        vmem((PARTS, 8, rows), F32),
        vmem((8, nk * rows), F32),
        vmem((8, rows), F32),
        vmem((8, nk * rows), F32),
        vmem((PARTS, rows, m * rows), F32),
        vmem((rows, nk * rows), BF16),
        vmem((rows, width), BF16),
        vmem((rows, width), BF16),
        vmem((rows, proj), BF16),
        vmem((rows, proj), BF16),
        vmem((m, PARTS * dk, rows), BF16),
        vmem((PARTS, PARTS * dk, m * rows), BF16),
        vmem((PARTS, rows, quarter), BF16),
        vmem((nk * rows, quarter), BF16),
        vmem((PARTS, dk, quarter), BF16),
        vmem((PARTS, dk, quarter), BF16),
        vmem((dk, quarter), BF16),
        vmem((PARTS, dk, quarter), BF16),
        pltpu.SemaphoreType.DMA((4,)),
    ]
    four, core, full = PARTS, 2 * m, nk
    for count in (four, four, full, full, core * PARTS, core, core, core, four, four, full, four, four):
        scratch += [pltpu.SemaphoreType.DMA((count,))] * 2
    macs = rows * proj * (2 * width + 2 * nk * rows) + PARTS * dk * nk * rows * quarter
    return pl.pallas_call(
        functools.partial(kernel, m),
        out_shape=(
            jax.ShapeDtypeStruct((rows, width), BF16),
            jax.ShapeDtypeStruct((dk, proj), F32),
        ),
        in_specs=[pl.BlockSpec(memory_space=pltpu.HBM)] * 4,
        out_specs=(pl.BlockSpec(memory_space=pltpu.VMEM), pl.BlockSpec(memory_space=pltpu.VMEM)),
        scratch_shapes=scratch,
        cost_estimate=pl.CostEstimate(flops=2 * macs, bytes_accessed=4 * rows * width + 2 * width * proj, transcendentals=rows * rows * nk),
        compiler_params=pltpu.CompilerParams(
            collective_id=0, has_side_effects=True, vmem_limit_bytes=(60 * 1024 - 256) * 1024
        ),
    )(embeddings, labels.reshape(1, rows), order, head_weight)


def solution(mesh):
    m = mesh.shape["key"] // PARTS
    return jax.shard_map(
        functools.partial(body, m),
        mesh=mesh,
        in_specs=(P(("shuf", "key"), None), P(("shuf", "key")), P(("shuf", "key"), None), P()),
        out_specs=(P(("shuf", "key"), None), P("key", None)),
        check_vma=False,
    )
```

```python
import functools

import jax
import jax.numpy as jnp
from jax import lax
from jax.experimental import pallas as pl
from jax.experimental.pallas import tpu as pltpu
from jax.sharding import PartitionSpec as P

MESH = pl.DeviceIdType.MESH
F32, BF16 = jnp.float32, jnp.bfloat16
exponent_divisor = 0.1
loss_scale = 64.0
epsilon = 1e-06
PARTS = 4


def nn(a, b):
    return lax.dot_general(a, b, (((1,), (0,)), ((), ())), preferred_element_type=F32)


def nt(a, b):
    return lax.dot_general(a, b, (((1,), (1,)), ((), ())), preferred_element_type=F32)


def tn(a, b):
    return lax.dot_general(a, b, (((0,), (0,)), ((), ())), preferred_element_type=F32)


def kernel(
    m, emb_hbm, lab_hbm, order_hbm, head_hbm, gemb_ref, ghead_ref,
    emb_ref, lab_ref, order_ref, head_ref,
    slot_ref, group_ref, labs_ref, labz_ref, labg_ref, wts_ref, wtg_ref, exp_ref, coef_ref,
    embs_ref, embz_ref, slope_ref, slopez_ref, embt_ref, embg_ref, slq_ref, slg_ref,
    hs_ref, hz_ref, qs_ref, qg_ref,
    in_sem, zs_sem, zr_sem, lzs_sem, lzr_sem, lgs_sem, lgr_sem, wgs_sem, wgr_sem,
    gs_sem, gr_sem, gfs_sem, gfr_sem, es_sem, er_sem, efs_sem, efr_sem,
    ts_sem, tr_sem, cs_sem, cr_sem, ss_sem, sr_sem, hs_sem, hr_sem, qs_sem, qr_sem,
):
    rows, width = emb_ref.shape
    slab = rows // PARTS
    nk = PARTS * m
    dk = width // nk
    quarter = head_ref.shape[1] // PARTS
    u = lax.axis_index("shuf")
    k = lax.axis_index("key")
    z, j = k // m, k % m

    def flip(a, du):
        for bit in (1, 2):
            if du & bit:
                a = a + bit - 2 * bit * ((a // bit) % 2)
        return a

    def ahead(dz):
        return (z + dz) % PARTS

    def behind(dz):
        return (z + PARTS - dz) % PARTS

    def there(du, dj):
        return flip(u, du), (j + dj) % m

    def origin(du, dj):
        return flip(u, du), (j + m - dj) % m

    def block_of(uj):
        return uj[0] * m + uj[1]

    def block_rows(ref, b):
        return ref.at[pl.ds(pl.multiple_of(b * rows, rows), rows)]

    def lanes_of(b):
        return pl.ds(pl.multiple_of(b * rows, rows), rows)

    def u_rows(ref, uu):
        return ref[pl.ds(pl.multiple_of(uu * (m * rows), m * rows), m * rows), :]

    def emb_cols(b):
        return embg_ref.at[b // m, :, lanes_of(b % m)]

    def plane_id(uj):
        return (uj[0], z * m + uj[1])

    def z_id(zz):
        return (u, zz * m + j)

    pending = []

    def send(src, dst, s_sem, r_sem, to):
        copy = pltpu.make_async_remote_copy(
            src_ref=src, dst_ref=dst, send_sem=s_sem, recv_sem=r_sem, device_id=to, device_id_type=MESH
        )
        copy.start()
        pending.append(copy)

    def arrived(dst, s_sem, r_sem, frm):
        pltpu.make_async_remote_copy(
            src_ref=dst, dst_ref=dst, send_sem=s_sem, recv_sem=r_sem, device_id=frm, device_id_type=MESH
        ).wait_recv()

    def drain(copies):
        for copy in copies:
            copy.wait_send()

    same_core = [(du, dj) for dj in range(m) for du in (0, 2)]
    plane = [(du, dj) for dj in range(m) for du in range(PARTS)]
    mine = block_of((u, j))

    loads = [
        pltpu.make_async_copy(src, dst, in_sem.at[i])
        for i, (src, dst) in enumerate(
            [(order_hbm, order_ref), (emb_hbm, emb_ref), (lab_hbm, lab_ref), (head_hbm, head_ref)]
        )
    ]
    for load in loads:
        load.start()
    barrier = pltpu.get_barrier_semaphore()
    for off in plane[1:]:
        pl.semaphore_signal(barrier, inc=1, device_id=plane_id(there(*off)), device_id_type=MESH)
    for dz in range(1, PARTS):
        pl.semaphore_signal(barrier, inc=1, device_id=z_id(ahead(dz)), device_id_type=MESH)

    sub = lax.broadcasted_iota(jnp.int32, (rows, rows), 0)
    lane = lax.broadcasted_iota(jnp.int32, (rows, rows), 1)
    eye = sub == lane
    loads[0].wait()
    place = sub == order_ref[...]
    place_bf = place.astype(F32).astype(BF16)

    def directions(x):
        projected = nn(x, head_ref[...])
        row_norm = jnp.sqrt(jnp.sum(projected * projected, axis=1, keepdims=True) + epsilon)
        return projected / row_norm, row_norm

    loads[2].wait()
    loads[1].wait()
    loads[3].wait()
    slot_ref[...] = tn(place_bf, directions(emb_ref[...])[0].astype(BF16)).astype(BF16)

    def column(row):
        return jnp.sum(jnp.where(eye, row, 0.0), axis=1, keepdims=True)

    def row_of(col):
        return jnp.sum(jnp.where(eye, col, 0.0), axis=0, keepdims=True)

    lab_col = column(lab_ref[...].astype(F32))
    lab_slot = jnp.sum(jnp.where(place, lab_col, 0.0), axis=0, keepdims=True)
    labs_ref[...] = jnp.broadcast_to(lab_slot, labs_ref.shape)
    pl.semaphore_wait(barrier, nk - 1 + PARTS - 1)

    def slab_rows(ref, i):
        return ref.at[pl.ds(pl.multiple_of(i * slab, slab), slab)]

    def group_slab(b, i):
        return group_ref.at[pl.ds(pl.multiple_of(b * rows + i * slab, slab), slab)]

    for dz in range(1, PARTS):
        zz = ahead(dz)
        send(slab_rows(slot_ref, zz), group_slab(mine, z), zs_sem.at[dz], zr_sem.at[dz], z_id(zz))
    for dz in range(1, PARTS):
        send(labs_ref, labz_ref.at[z], lzs_sem.at[dz], lzr_sem.at[dz], z_id(ahead(dz)))
    own = pl.multiple_of(mine * rows + z * slab, slab)
    own_slot = pl.multiple_of(z * slab, slab)
    group_ref[pl.ds(own, slab), :] = slot_ref[pl.ds(own_slot, slab), :]
    labz_ref[z] = labs_ref[...]

    def extract(buf_ref):
        lanes = lax.broadcasted_iota(jnp.int32, (8, rows), 1) // slab
        out = jnp.zeros((8, rows), F32)
        for i in range(PARTS):
            moved = pltpu.roll(buf_ref[i], ((i + PARTS - z) % PARTS) * slab, 1)
            out = jnp.where(lanes == i, moved, out)
        return out

    for dz in range(PARTS):
        piece = group_slab(mine, behind(dz))
        if dz:
            arrived(piece, zs_sem.at[dz], zr_sem.at[dz], z_id(behind(dz)))
        for i, off in enumerate(same_core):
            if i:
                n = i * PARTS + dz
                send(piece, piece, gs_sem.at[n], gr_sem.at[n], plane_id(there(*off)))
        if dz == 0:
            embs_ref[...] = tn(place_bf, emb_ref[...]).astype(BF16)
            embz_ref[pl.ds(own_slot, slab), :] = embs_ref[pl.ds(own_slot, slab), :]
    for dz in range(1, PARTS):
        zz = ahead(dz)
        send(slab_rows(embs_ref, zz), slab_rows(embz_ref, z), cs_sem.at[dz], cr_sem.at[dz], z_id(zz))
    partner = there(1, 0)
    send(block_rows(group_ref, mine), block_rows(group_ref, mine), gfs_sem.at[0], gfr_sem.at[0], plane_id(partner))
    for dz in range(1, PARTS):
        arrived(labz_ref.at[behind(dz)], lzs_sem.at[dz], lzr_sem.at[dz], z_id(behind(dz)))
    own_label = extract(labz_ref)
    labg_ref[:, lanes_of(mine)] = own_label
    for i, off in enumerate(plane):
        if i:
            send(labg_ref.at[:, lanes_of(mine)], labg_ref.at[:, lanes_of(mine)], lgs_sem.at[i], lgr_sem.at[i], plane_id(there(*off)))

    anchors = group_ref[pl.ds(pl.multiple_of(mine * rows, rows), rows), :]
    anchor_col = column(own_label[0:1, :])
    wide = m * rows
    row_id = lax.broadcasted_iota(jnp.int32, (rows, wide), 0) + mine * rows
    lane_id = lax.broadcasted_iota(jnp.int32, (rows, wide), 1)

    def exponent_of(uu, own):
        value = jnp.exp(nt(anchors, u_rows(group_ref, uu)) / exponent_divisor)
        if own:
            value = jnp.where(row_id == lane_id + uu * wide, 0.0, value)
        exp_ref[uu] = value
        return jnp.sum(value, axis=1, keepdims=True)

    def positive_of(uu):
        same = jnp.logical_and(
            anchor_col == labg_ref[0:1, uu * wide : (uu + 1) * wide], row_id != lane_id + uu * wide
        )
        return jnp.where(same, 1.0, 0.0)

    def gathered(du):
        for i, off in enumerate(same_core):
            if i and off[0] == du:
                frm = origin(*off)
                b = block_of(frm)
                for dz in range(PARTS):
                    n = i * PARTS + dz
                    arrived(group_slab(b, behind(dz)), gs_sem.at[n], gr_sem.at[n], plane_id(frm))
                send(block_rows(group_ref, b), block_rows(group_ref, b), gfs_sem.at[i], gfr_sem.at[i], plane_id(partner))

    def forwarded(du):
        for i, off in enumerate(same_core):
            if off[0] == du:
                uj = origin(*off)
                b = block_of((flip(uj[0], 1), uj[1]))
                yield i, b

    gathered(0)
    gathered(2)
    total = exponent_of(u, True)
    total = total + exponent_of(flip(u, 2), False)
    for i, off in enumerate(plane):
        if i:
            frm = origin(*off)
            arrived(labg_ref.at[:, lanes_of(block_of(frm))], lgs_sem.at[i], lgr_sem.at[i], plane_id(frm))
    counts = jnp.sum(positive_of(0), axis=1, keepdims=True)
    for uu in range(1, PARTS):
        counts = counts + jnp.sum(positive_of(uu), axis=1, keepdims=True)
    for du in (0, 2):
        for i, b in forwarded(du):
            arrived(block_rows(group_ref, b), gfs_sem.at[i], gfr_sem.at[i], plane_id(partner))
        total = total + exponent_of(flip(u, du + 1), False)
    totals = total
    floor_count = jnp.maximum(counts, 1.0)
    soft = loss_scale * counts / (floor_count * totals)
    pos = loss_scale / floor_count
    first_row = lax.broadcasted_iota(jnp.int32, (8, rows), 0) == 0
    wts_ref[...] = jnp.where(first_row, row_of(soft), row_of(pos))
    wtg_ref[:, lanes_of(mine)] = wts_ref[...]
    for i, off in enumerate(plane):
        if i:
            send(wts_ref, wtg_ref.at[:, lanes_of(mine)], wgs_sem.at[i], wgr_sem.at[i], plane_id(there(*off)))

    for dz in range(1, PARTS):
        arrived(slab_rows(embz_ref, behind(dz)), cs_sem.at[dz], cr_sem.at[dz], z_id(behind(dz)))
    turned = embz_ref[...].T
    for jj in range(m):
        for zz in range(PARTS):
            start = (zz * m + jj) * dk
            embt_ref[jj, zz * dk : (zz + 1) * dk, :] = turned[start : start + dk, :]
    for i, off in enumerate(same_core):
        if i:
            to = there(*off)
            send(embt_ref.at[to[1]], emb_cols(mine), es_sem.at[i], er_sem.at[i], plane_id(to))
    embg_ref[u, :, lanes_of(j)] = embt_ref[j]
    send(emb_cols(mine), emb_cols(mine), efs_sem.at[0], efr_sem.at[0], plane_id(partner))
    direction, row_norm = directions(embz_ref[...])

    for i, off in enumerate(plane):
        if i:
            frm = origin(*off)
            arrived(wtg_ref.at[:, lanes_of(block_of(frm))], wgs_sem.at[i], wgr_sem.at[i], plane_id(frm))
    for uu in range(PARTS):
        cols = slice(uu * wide, (uu + 1) * wide)
        coefficient = (soft + wtg_ref[0:1, cols]) * exp_ref[uu] - (pos + wtg_ref[1:2, cols]) * positive_of(uu)
        coef_ref[:, cols] = coefficient.astype(BF16)
    pull = nn(coef_ref[...], group_ref[...]) / exponent_divisor
    slopes = (pull - direction * jnp.sum(direction * pull, axis=1, keepdims=True)) / row_norm
    slopes = slopes.astype(BF16)
    slope_ref[...] = slopes
    for uu in range(PARTS):
        slq_ref[uu] = slopes[:, uu * quarter : (uu + 1) * quarter]
    for i, off in enumerate(plane):
        if i:
            to = there(*off)
            send(slq_ref.at[to[0]], block_rows(slg_ref, mine), ss_sem.at[i], sr_sem.at[i], plane_id(to))
    slg_ref[pl.ds(pl.multiple_of(mine * rows, rows), rows), :] = slq_ref[u]
    for dz in range(1, PARTS):
        zz = ahead(dz)
        send(slab_rows(slope_ref, zz), slab_rows(slopez_ref, z), ts_sem.at[dz], tr_sem.at[dz], z_id(zz))
    slopez_ref[pl.ds(own_slot, slab), :] = slope_ref[pl.ds(own_slot, slab), :]
    for i, off in enumerate(same_core):
        if i:
            frm = origin(*off)
            b = block_of(frm)
            arrived(emb_cols(b), es_sem.at[i], er_sem.at[i], plane_id(frm))
            send(emb_cols(b), emb_cols(b), efs_sem.at[i], efr_sem.at[i], plane_id(partner))
    part = None
    for du in range(PARTS):
        if du % 2:
            for i, b in forwarded(du - 1):
                arrived(emb_cols(b), efs_sem.at[i], efr_sem.at[i], plane_id(partner))
        for i, off in enumerate(plane):
            if i and off[0] == du:
                frm = origin(*off)
                arrived(block_rows(slg_ref, block_of(frm)), ss_sem.at[i], sr_sem.at[i], plane_id(frm))
        term = nn(embg_ref[flip(u, du)], u_rows(slg_ref, flip(u, du)))
        part = term if part is None else part + term
    earlier = len(pending)
    hs_ref[...] = part.astype(BF16).reshape(hs_ref.shape)
    for dz in range(1, PARTS):
        zz = ahead(dz)
        send(hs_ref.at[zz], hz_ref.at[z], hs_sem.at[dz], hr_sem.at[dz], z_id(zz))
    hz_ref[z] = hs_ref[z]
    for dz in range(1, PARTS):
        frm = behind(dz)
        arrived(slab_rows(slopez_ref, frm), ts_sem.at[dz], tr_sem.at[dz], z_id(frm))
    drain(pending[:earlier])
    gemb_ref[...] = nt(nn(place_bf, slopez_ref[...]).astype(BF16), head_ref[...]).astype(BF16)
    for dz in range(1, PARTS):
        arrived(hz_ref.at[behind(dz)], hs_sem.at[dz], hr_sem.at[dz], z_id(behind(dz)))
    part = hz_ref[0].astype(F32)
    for zz in range(1, PARTS):
        part = part + hz_ref[zz].astype(F32)
    qs_ref[...] = (part / loss_scale).astype(BF16)
    for du in range(1, PARTS):
        send(qs_ref, qg_ref.at[u], qs_sem.at[du], qr_sem.at[du], plane_id(there(du, 0)))
    qg_ref[u] = qs_ref[...]
    for du in range(1, PARTS):
        frm = origin(du, 0)
        arrived(qg_ref.at[frm[0]], qs_sem.at[du], qr_sem.at[du], plane_id(frm))
    for uu in range(PARTS):
        ghead_ref[:, uu * quarter : (uu + 1) * quarter] = qg_ref[uu].astype(F32)
    drain(pending[earlier:])


def body(m, embeddings, labels, order, head_weight):
    rows, width = embeddings.shape
    proj = head_weight.shape[1]
    nk = PARTS * m
    dk = width // nk
    quarter = proj // PARTS
    vmem = pltpu.VMEM
    scratch = [
        vmem((rows, width), BF16),
        vmem((1, rows), jnp.int32),
        vmem((1, rows), jnp.int32),
        vmem((width, proj), BF16),
        vmem((rows, proj), BF16),
        vmem((nk * rows, proj), BF16),
        vmem((8, rows), F32),
        vmem((PARTS, 8, rows), F32),
        vmem((8, nk * rows), F32),
        vmem((8, rows), F32),
        vmem((8, nk * rows), F32),
        vmem((PARTS, rows, m * rows), F32),
        vmem((rows, nk * rows), BF16),
        vmem((rows, width), BF16),
        vmem((rows, width), BF16),
        vmem((rows, proj), BF16),
        vmem((rows, proj), BF16),
        vmem((m, PARTS * dk, rows), BF16),
        vmem((PARTS, PARTS * dk, m * rows), BF16),
        vmem((PARTS, rows, quarter), BF16),
        vmem((nk * rows, quarter), BF16),
        vmem((PARTS, dk, quarter), BF16),
        vmem((PARTS, dk, quarter), BF16),
        vmem((dk, quarter), BF16),
        vmem((PARTS, dk, quarter), BF16),
        pltpu.SemaphoreType.DMA((4,)),
    ]
    four, core, full = PARTS, 2 * m, nk
    for count in (four, four, full, full, core * PARTS, core, core, core, four, four, full, four, four):
        scratch += [pltpu.SemaphoreType.DMA((count,))] * 2
    macs = rows * proj * (2 * width + 2 * nk * rows) + PARTS * dk * nk * rows * quarter
    return pl.pallas_call(
        functools.partial(kernel, m),
        out_shape=(
            jax.ShapeDtypeStruct((rows, width), BF16),
            jax.ShapeDtypeStruct((dk, proj), F32),
        ),
        in_specs=[pl.BlockSpec(memory_space=pltpu.HBM)] * 4,
        out_specs=(pl.BlockSpec(memory_space=pltpu.VMEM), pl.BlockSpec(memory_space=pltpu.VMEM)),
        scratch_shapes=scratch,
        cost_estimate=pl.CostEstimate(flops=2 * macs, bytes_accessed=4 * rows * width + 2 * width * proj, transcendentals=rows * rows * nk),
        compiler_params=pltpu.CompilerParams(
            collective_id=0, has_side_effects=True, vmem_limit_bytes=(60 * 1024 - 640) * 1024
        ),
    )(embeddings, labels.reshape(1, rows), order, head_weight)


def solution(mesh):
    m = mesh.shape["key"] // PARTS
    return jax.shard_map(
        functools.partial(body, m),
        mesh=mesh,
        in_specs=(P(("shuf", "key"), None), P(("shuf", "key")), P(("shuf", "key"), None), P()),
        out_specs=(P(("shuf", "key"), None), P("key", None)),
        check_vma=False,
    )
```

```python
import functools

import jax
import jax.numpy as jnp
from jax import lax
from jax.experimental import pallas as pl
from jax.experimental.pallas import tpu as pltpu
from jax.sharding import PartitionSpec as P

MESH = pl.DeviceIdType.MESH
F32, BF16 = jnp.float32, jnp.bfloat16
exponent_divisor = 0.1
loss_scale = 64.0
epsilon = 1e-06
PARTS = 4


def nn(a, b):
    return lax.dot_general(a, b, (((1,), (0,)), ((), ())), preferred_element_type=F32)


def nt(a, b):
    return lax.dot_general(a, b, (((1,), (1,)), ((), ())), preferred_element_type=F32)


def tn(a, b):
    return lax.dot_general(a, b, (((0,), (0,)), ((), ())), preferred_element_type=F32)


def kernel(
    m, emb_hbm, lab_hbm, order_hbm, head_hbm, gemb_ref, ghead_ref,
    emb_ref, lab_ref, order_ref, head_ref,
    slot_ref, group_ref, labs_ref, labz_ref, labg_ref, wts_ref, wtg_ref, exp_ref, coef_ref,
    embs_ref, embz_ref, slope_ref, slopez_ref, embt_ref, embg_ref, slq_ref, slg_ref,
    hs_ref, hz_ref, qs_ref, qg_ref,
    in_sem, zs_sem, zr_sem, lzs_sem, lzr_sem, lgs_sem, lgr_sem, wgs_sem, wgr_sem,
    gs_sem, gr_sem, gfs_sem, gfr_sem, es_sem, er_sem, efs_sem, efr_sem,
    ts_sem, tr_sem, cs_sem, cr_sem, ss_sem, sr_sem, hs_sem, hr_sem, qs_sem, qr_sem,
):
    rows, width = emb_ref.shape
    slab = rows // PARTS
    nk = PARTS * m
    dk = width // nk
    quarter = head_ref.shape[1] // PARTS
    u = lax.axis_index("shuf")
    k = lax.axis_index("key")
    z, j = k // m, k % m

    def flip(a, du):
        for bit in (1, 2):
            if du & bit:
                a = a + bit - 2 * bit * ((a // bit) % 2)
        return a

    def ahead(dz):
        return (z + dz) % PARTS

    def behind(dz):
        return (z + PARTS - dz) % PARTS

    def there(du, dj):
        return flip(u, du), (j + dj) % m

    def origin(du, dj):
        return flip(u, du), (j + m - dj) % m

    def block_of(uj):
        return uj[0] * m + uj[1]

    def block_rows(ref, b):
        return ref.at[pl.ds(pl.multiple_of(b * rows, rows), rows)]

    def lanes_of(b):
        return pl.ds(pl.multiple_of(b * rows, rows), rows)

    def u_rows(ref, uu):
        return ref[pl.ds(pl.multiple_of(uu * (m * rows), m * rows), m * rows), :]

    def emb_cols(b):
        return embg_ref.at[b // m, :, lanes_of(b % m)]

    def plane_id(uj):
        return (uj[0], z * m + uj[1])

    def z_id(zz):
        return (u, zz * m + j)

    pending = []

    def send(src, dst, s_sem, r_sem, to):
        copy = pltpu.make_async_remote_copy(
            src_ref=src, dst_ref=dst, send_sem=s_sem, recv_sem=r_sem, device_id=to, device_id_type=MESH
        )
        copy.start()
        pending.append(copy)

    def arrived(dst, s_sem, r_sem, frm):
        pltpu.make_async_remote_copy(
            src_ref=dst, dst_ref=dst, send_sem=s_sem, recv_sem=r_sem, device_id=frm, device_id_type=MESH
        ).wait_recv()

    def drain(copies):
        for copy in copies:
            copy.wait_send()

    same_core = [(du, dj) for dj in range(m) for du in (0, 2)]
    plane = [(du, dj) for dj in range(m) for du in range(PARTS)]
    mine = block_of((u, j))

    loads = [
        pltpu.make_async_copy(src, dst, in_sem.at[i])
        for i, (src, dst) in enumerate(
            [(order_hbm, order_ref), (emb_hbm, emb_ref), (lab_hbm, lab_ref), (head_hbm, head_ref)]
        )
    ]
    for load in loads:
        load.start()
    barrier = pltpu.get_barrier_semaphore()
    for off in plane[1:]:
        pl.semaphore_signal(barrier, inc=1, device_id=plane_id(there(*off)), device_id_type=MESH)
    for dz in range(1, PARTS):
        pl.semaphore_signal(barrier, inc=1, device_id=z_id(ahead(dz)), device_id_type=MESH)

    sub = lax.broadcasted_iota(jnp.int32, (rows, rows), 0)
    lane = lax.broadcasted_iota(jnp.int32, (rows, rows), 1)
    eye = sub == lane
    loads[0].wait()
    place = sub == order_ref[...]
    place_bf = place.astype(F32).astype(BF16)

    def directions(x):
        projected = nn(x, head_ref[...])
        row_norm = jnp.sqrt(jnp.sum(projected * projected, axis=1, keepdims=True) + epsilon)
        return projected / row_norm, row_norm

    loads[2].wait()
    loads[1].wait()
    loads[3].wait()
    slot_ref[...] = tn(place_bf, directions(emb_ref[...])[0].astype(BF16)).astype(BF16)

    def column(row):
        return jnp.sum(jnp.where(eye, row, 0.0), axis=1, keepdims=True)

    def row_of(col):
        return jnp.sum(jnp.where(eye, col, 0.0), axis=0, keepdims=True)

    lab_col = column(lab_ref[...].astype(F32))
    lab_slot = jnp.sum(jnp.where(place, lab_col, 0.0), axis=0, keepdims=True)
    labs_ref[...] = jnp.broadcast_to(lab_slot, labs_ref.shape)
    pl.semaphore_wait(barrier, nk - 1 + PARTS - 1)

    def slab_rows(ref, i):
        return ref.at[pl.ds(pl.multiple_of(i * slab, slab), slab)]

    def group_slab(b, i):
        return group_ref.at[pl.ds(pl.multiple_of(b * rows + i * slab, slab), slab)]

    for dz in range(1, PARTS):
        zz = ahead(dz)
        send(slab_rows(slot_ref, zz), group_slab(mine, z), zs_sem.at[dz], zr_sem.at[dz], z_id(zz))
    for dz in range(1, PARTS):
        send(labs_ref, labz_ref.at[z], lzs_sem.at[dz], lzr_sem.at[dz], z_id(ahead(dz)))
    own = pl.multiple_of(mine * rows + z * slab, slab)
    own_slot = pl.multiple_of(z * slab, slab)
    group_ref[pl.ds(own, slab), :] = slot_ref[pl.ds(own_slot, slab), :]
    labz_ref[z] = labs_ref[...]

    def extract(buf_ref):
        lanes = lax.broadcasted_iota(jnp.int32, (8, rows), 1) // slab
        out = jnp.zeros((8, rows), F32)
        for i in range(PARTS):
            moved = pltpu.roll(buf_ref[i], ((i + PARTS - z) % PARTS) * slab, 1)
            out = jnp.where(lanes == i, moved, out)
        return out

    for dz in range(PARTS):
        piece = group_slab(mine, behind(dz))
        if dz:
            arrived(piece, zs_sem.at[dz], zr_sem.at[dz], z_id(behind(dz)))
        for i, off in enumerate(same_core):
            if i:
                n = i * PARTS + dz
                send(piece, piece, gs_sem.at[n], gr_sem.at[n], plane_id(there(*off)))
        if dz == 0:
            embs_ref[...] = tn(place_bf, emb_ref[...]).astype(BF16)
            embz_ref[pl.ds(own_slot, slab), :] = embs_ref[pl.ds(own_slot, slab), :]
    for dz in range(1, PARTS):
        zz = ahead(dz)
        send(slab_rows(embs_ref, zz), slab_rows(embz_ref, z), cs_sem.at[dz], cr_sem.at[dz], z_id(zz))
    partner = there(1, 0)
    send(block_rows(group_ref, mine), block_rows(group_ref, mine), gfs_sem.at[0], gfr_sem.at[0], plane_id(partner))
    for dz in range(1, PARTS):
        arrived(labz_ref.at[behind(dz)], lzs_sem.at[dz], lzr_sem.at[dz], z_id(behind(dz)))
    own_label = extract(labz_ref)
    labg_ref[:, lanes_of(mine)] = own_label
    for i, off in enumerate(plane):
        if i:
            send(labg_ref.at[:, lanes_of(mine)], labg_ref.at[:, lanes_of(mine)], lgs_sem.at[i], lgr_sem.at[i], plane_id(there(*off)))

    anchors = group_ref[pl.ds(pl.multiple_of(mine * rows, rows), rows), :]
    anchor_col = column(own_label[0:1, :])
    wide = m * rows
    row_id = lax.broadcasted_iota(jnp.int32, (rows, wide), 0) + mine * rows
    lane_id = lax.broadcasted_iota(jnp.int32, (rows, wide), 1)

    def exponent_of(uu, own):
        value = jnp.exp(nt(anchors, u_rows(group_ref, uu)) / exponent_divisor)
        if own:
            value = jnp.where(row_id == lane_id + uu * wide, 0.0, value)
        exp_ref[uu] = value
        return jnp.sum(value, axis=1, keepdims=True)

    def positive_of(uu):
        same = jnp.logical_and(
            anchor_col == labg_ref[0:1, uu * wide : (uu + 1) * wide], row_id != lane_id + uu * wide
        )
        return jnp.where(same, 1.0, 0.0)

    def gathered(du):
        for i, off in enumerate(same_core):
            if i and off[0] == du:
                frm = origin(*off)
                b = block_of(frm)
                for dz in range(PARTS):
                    n = i * PARTS + dz
                    arrived(group_slab(b, behind(dz)), gs_sem.at[n], gr_sem.at[n], plane_id(frm))
                send(block_rows(group_ref, b), block_rows(group_ref, b), gfs_sem.at[i], gfr_sem.at[i], plane_id(partner))

    def forwarded(du):
        for i, off in enumerate(same_core):
            if off[0] == du:
                uj = origin(*off)
                b = block_of((flip(uj[0], 1), uj[1]))
                yield i, b

    gathered(0)
    gathered(2)
    total = exponent_of(u, True)
    total = total + exponent_of(flip(u, 2), False)
    for i, off in enumerate(plane):
        if i:
            frm = origin(*off)
            arrived(labg_ref.at[:, lanes_of(block_of(frm))], lgs_sem.at[i], lgr_sem.at[i], plane_id(frm))
    counts = jnp.sum(positive_of(0), axis=1, keepdims=True)
    for uu in range(1, PARTS):
        counts = counts + jnp.sum(positive_of(uu), axis=1, keepdims=True)
    for du in (0, 2):
        for i, b in forwarded(du):
            arrived(block_rows(group_ref, b), gfs_sem.at[i], gfr_sem.at[i], plane_id(partner))
        total = total + exponent_of(flip(u, du + 1), False)
    totals = total
    floor_count = jnp.maximum(counts, 1.0)
    soft = loss_scale * counts / (floor_count * totals)
    pos = loss_scale / floor_count
    first_row = lax.broadcasted_iota(jnp.int32, (8, rows), 0) == 0
    wts_ref[...] = jnp.where(first_row, row_of(soft), row_of(pos))
    wtg_ref[:, lanes_of(mine)] = wts_ref[...]
    for i, off in enumerate(plane):
        if i:
            send(wts_ref, wtg_ref.at[:, lanes_of(mine)], wgs_sem.at[i], wgr_sem.at[i], plane_id(there(*off)))

    for dz in range(1, PARTS):
        arrived(slab_rows(embz_ref, behind(dz)), cs_sem.at[dz], cr_sem.at[dz], z_id(behind(dz)))
    turned = embz_ref[...].T
    for jj in range(m):
        for zz in range(PARTS):
            start = (zz * m + jj) * dk
            embt_ref[jj, zz * dk : (zz + 1) * dk, :] = turned[start : start + dk, :]
    for i, off in enumerate(same_core):
        if i:
            to = there(*off)
            send(embt_ref.at[to[1]], emb_cols(mine), es_sem.at[i], er_sem.at[i], plane_id(to))
    embg_ref[u, :, lanes_of(j)] = embt_ref[j]
    send(emb_cols(mine), emb_cols(mine), efs_sem.at[0], efr_sem.at[0], plane_id(partner))
    direction, row_norm = directions(embz_ref[...])

    for i, off in enumerate(plane):
        if i:
            frm = origin(*off)
            arrived(wtg_ref.at[:, lanes_of(block_of(frm))], wgs_sem.at[i], wgr_sem.at[i], plane_id(frm))
    for uu in range(PARTS):
        cols = slice(uu * wide, (uu + 1) * wide)
        coefficient = (soft + wtg_ref[0:1, cols]) * exp_ref[uu] - (pos + wtg_ref[1:2, cols]) * positive_of(uu)
        coef_ref[:, cols] = coefficient.astype(BF16)
    pull = nn(coef_ref[...], group_ref[...]) / exponent_divisor
    slopes = (pull - direction * jnp.sum(direction * pull, axis=1, keepdims=True)) / row_norm
    slopes = slopes.astype(BF16)
    slope_ref[...] = slopes
    for uu in range(PARTS):
        slq_ref[uu] = slopes[:, uu * quarter : (uu + 1) * quarter]
    for i, off in enumerate(plane):
        if i:
            to = there(*off)
            send(slq_ref.at[to[0]], block_rows(slg_ref, mine), ss_sem.at[i], sr_sem.at[i], plane_id(to))
    slg_ref[pl.ds(pl.multiple_of(mine * rows, rows), rows), :] = slq_ref[u]
    for dz in range(1, PARTS):
        zz = ahead(dz)
        send(slab_rows(slope_ref, zz), slab_rows(slopez_ref, z), ts_sem.at[dz], tr_sem.at[dz], z_id(zz))
    slopez_ref[pl.ds(own_slot, slab), :] = slope_ref[pl.ds(own_slot, slab), :]
    for i, off in enumerate(same_core):
        if i:
            frm = origin(*off)
            b = block_of(frm)
            arrived(emb_cols(b), es_sem.at[i], er_sem.at[i], plane_id(frm))
            send(emb_cols(b), emb_cols(b), efs_sem.at[i], efr_sem.at[i], plane_id(partner))
    part = None
    for du in range(PARTS):
        if du % 2:
            for i, b in forwarded(du - 1):
                arrived(emb_cols(b), efs_sem.at[i], efr_sem.at[i], plane_id(partner))
        for i, off in enumerate(plane):
            if i and off[0] == du:
                frm = origin(*off)
                arrived(block_rows(slg_ref, block_of(frm)), ss_sem.at[i], sr_sem.at[i], plane_id(frm))
        term = nn(embg_ref[flip(u, du)], u_rows(slg_ref, flip(u, du)))
        part = term if part is None else part + term
    earlier = len(pending)
    hs_ref[...] = part.astype(BF16).reshape(hs_ref.shape)
    for dz in range(1, PARTS):
        zz = ahead(dz)
        send(hs_ref.at[zz], hz_ref.at[z], hs_sem.at[dz], hr_sem.at[dz], z_id(zz))
    hz_ref[z] = hs_ref[z]
    for dz in range(1, PARTS):
        frm = behind(dz)
        arrived(slab_rows(slopez_ref, frm), ts_sem.at[dz], tr_sem.at[dz], z_id(frm))
    drain(pending[:earlier])
    gemb_ref[...] = nt(nn(place_bf, slopez_ref[...]).astype(BF16), head_ref[...]).astype(BF16)
    for dz in range(1, PARTS):
        arrived(hz_ref.at[behind(dz)], hs_sem.at[dz], hr_sem.at[dz], z_id(behind(dz)))
    part = hz_ref[0].astype(F32)
    for zz in range(1, PARTS):
        part = part + hz_ref[zz].astype(F32)
    qs_ref[...] = (part / loss_scale).astype(BF16)
    for du in range(1, PARTS):
        send(qs_ref, qg_ref.at[u], qs_sem.at[du], qr_sem.at[du], plane_id(there(du, 0)))
    qg_ref[u] = qs_ref[...]
    for du in range(1, PARTS):
        frm = origin(du, 0)
        arrived(qg_ref.at[frm[0]], qs_sem.at[du], qr_sem.at[du], plane_id(frm))
    for uu in range(PARTS):
        ghead_ref[:, uu * quarter : (uu + 1) * quarter] = qg_ref[uu].astype(F32)
    drain(pending[earlier:])


def body(m, embeddings, labels, order, head_weight):
    rows, width = embeddings.shape
    proj = head_weight.shape[1]
    nk = PARTS * m
    dk = width // nk
    quarter = proj // PARTS
    vmem = pltpu.VMEM
    scratch = [
        vmem((rows, width), BF16),
        vmem((1, rows), jnp.int32),
        vmem((1, rows), jnp.int32),
        vmem((width, proj), BF16),
        vmem((rows, proj), BF16),
        vmem((nk * rows, proj), BF16),
        vmem((8, rows), F32),
        vmem((PARTS, 8, rows), F32),
        vmem((8, nk * rows), F32),
        vmem((8, rows), F32),
        vmem((8, nk * rows), F32),
        vmem((PARTS, rows, m * rows), F32),
        vmem((rows, nk * rows), BF16),
        vmem((rows, width), BF16),
        vmem((rows, width), BF16),
        vmem((rows, proj), BF16),
        vmem((rows, proj), BF16),
        vmem((m, PARTS * dk, rows), BF16),
        vmem((PARTS, PARTS * dk, m * rows), BF16),
        vmem((PARTS, rows, quarter), BF16),
        vmem((nk * rows, quarter), BF16),
        vmem((PARTS, dk, quarter), BF16),
        vmem((PARTS, dk, quarter), BF16),
        vmem((dk, quarter), BF16),
        vmem((PARTS, dk, quarter), BF16),
        pltpu.SemaphoreType.DMA((4,)),
    ]
    four, core, full = PARTS, 2 * m, nk
    for count in (four, four, full, full, core * PARTS, core, core, core, four, four, full, four, four):
        scratch += [pltpu.SemaphoreType.DMA((count,))] * 2
    macs = rows * proj * (2 * width + 2 * nk * rows) + PARTS * dk * nk * rows * quarter
    return pl.pallas_call(
        functools.partial(kernel, m),
        out_shape=(
            jax.ShapeDtypeStruct((rows, width), BF16),
            jax.ShapeDtypeStruct((dk, proj), F32),
        ),
        in_specs=[pl.BlockSpec(memory_space=pltpu.HBM)] * 4,
        out_specs=(pl.BlockSpec(memory_space=pltpu.VMEM), pl.BlockSpec(memory_space=pltpu.VMEM)),
        scratch_shapes=scratch,
        cost_estimate=pl.CostEstimate(flops=2 * macs, bytes_accessed=4 * rows * width + 2 * width * proj, transcendentals=rows * rows * nk),
        compiler_params=pltpu.CompilerParams(
            collective_id=0, has_side_effects=True, vmem_limit_bytes=59 * 1024 * 1024
        ),
    )(embeddings, labels.reshape(1, rows), order, head_weight)


def solution(mesh):
    m = mesh.shape["key"] // PARTS
    return jax.shard_map(
        functools.partial(body, m),
        mesh=mesh,
        in_specs=(P(("shuf", "key"), None), P(("shuf", "key")), P(("shuf", "key"), None), P()),
        out_specs=(P(("shuf", "key"), None), P("key", None)),
        check_vma=False,
    )
```
